512 devices in a mesh: ctx: 32 (over z, y_lo, core), tp: 4 (over x), var: 4 (over y_hi).
Axes of the slice: x: 4, y: 8 (y_hi: 4, y_lo: 2; y = y_hi * 2 + y_lo), z: 8, core: 2. Of those that a mesh axis runs over, the one named last changes fastest.
Arguments:
- context_kv: bfloat16 [2, 8192, 8192], P(None, ('ctx', 'var'), 'tp'), may hold values from -14 to 14
- queries: bfloat16 [128, 32, 8192], P(('ctx', 'var'), None, 'tp'), may hold values from -14 to 14
- cont_keys: bfloat16 [128, 32, 8192], P(('ctx', 'var'), None, 'tp'), may hold values from -6 to 6
- hyena_inputs: bfloat16 [3, 128, 32, 8192], P(None, ('ctx', 'var'), None, 'tp'), may hold values from -6 to 6
- hyena_state: bfloat16 [128, 8192], P(('ctx', 'var'), 'tp'), may hold values from -6 to 6
- hyena_filter: float32 [8192, 128], P('tp'), may hold values from -0.6 to 0.6
- filter_skip: float32 [8192], P('tp'), may hold values from -3 to 3
- unembed: bfloat16 [8192, 512], P('tp'), may hold values from -21 to 21
- ref_bases: int32 [32], replicated, may hold values from 0 to 3
- variant_pos: int32 [128], P(('ctx', 'var')), may hold values from 0 to 31
- allele_ids: int32 [128], P(('ctx', 'var')), may hold values from 0 to 3
- cont_lengths: int32 [128], P(('ctx', 'var')), may hold values from 16 to 32, as said below
Outputs:
- hyena_out: bfloat16 [128, 32, 8192], P(('ctx', 'var'), None, 'tp')
- log_probs: float32 [128, 32], P(('ctx', 'var'))
- variant_scores: float32 [128], P(('ctx', 'var'))
The draws below stay inside these ranges and needn't reach their ends.
Inputs may be any that keep to these rules, and one draw needn't show every extreme that they name: `variant_pos`: position of the variant inside its continuation. `allele_ids`: base codes of the alleles. `cont_lengths`: some continuation has 32 scored bases and some has 16.
All inputs are finite; a program needn't handle non-finite values.
Results may differ from the reference program's by a relative error of at most 0.0065.
Values may be sent and summed in bfloat16 or wider, within the bound.
A program may use at most 192 MiB of HBM per device.

```python
import jax
import jax.numpy as jnp
from jax import lax

D = 8192
HEADS = 64
HEAD_DIM = 128
FLEN = 128
VOCAB = 512
CONT = 32
CTX_DEV = 256
CTX = 8192
VARIANTS = 128
N_CTX = 32


def draw_queries(key, part):
    key = jax.random.fold_in(key, 5)
    values = jnp.clip(jax.random.normal(key, (VARIANTS, CONT, D), jnp.float32), -6.0, 6.0) * 1.4
    return values.astype(jnp.bfloat16)


def draw_context_kv(key, part):
    key = jax.random.fold_in(key, 9)
    key_part, value_part = jax.random.split(key)
    keys_drawn = jnp.clip(jax.random.normal(key_part, (CTX, D), jnp.float32), -6.0, 6.0) * 1.4
    values_drawn = jnp.clip(jax.random.normal(value_part, (CTX, D), jnp.float32), -6.0, 6.0)
    return jnp.stack([keys_drawn, values_drawn]).astype(jnp.bfloat16)


def draw_hyena_filter(key, part):
    key = jax.random.fold_in(key, 13)
    rate_key, tap_key = jax.random.split(key)
    rates = jnp.exp(jax.random.uniform(rate_key, (D, 1), jnp.float32, jnp.log(0.002), jnp.log(0.08)))
    taps = jnp.clip(jax.random.normal(tap_key, (D, FLEN), jnp.float32), -4.0, 4.0)
    decay = jnp.exp(-rates * jnp.arange(FLEN, dtype=jnp.float32)[None, :])
    return (0.15 * taps * decay).astype(jnp.float32)


def draw_unembed(key, part):
    key = jax.random.fold_in(key, 17)
    entry_key = jax.random.fold_in(key, 0)
    values = jnp.clip(jax.random.normal(entry_key, (D, VOCAB), jnp.float32), -4.0, 4.0) * 0.3
    return values.astype(jnp.bfloat16)


def draw_cont_lengths(key, part):
    key = jax.random.fold_in(key, 21)
    length_key, order_key = jax.random.split(key)
    lengths = jax.random.randint(length_key, (VARIANTS,), CONT // 2, CONT + 1, jnp.int32)
    order = jax.random.permutation(order_key, VARIANTS)
    lengths = lengths.at[order[0]].set(CONT).at[order[1]].set(CONT // 2)
    return lengths.astype(jnp.int32)


def place_ends(values, key, smallest, high):
    longest = values.shape.index(max(values.shape))
    spots = []
    for shift in (0, 1):
        where = [jax.random.randint(jax.random.fold_in(key, axis), (), 0, length) for axis, length in enumerate(values.shape)]
        where[longest] = (where[longest] + shift) % values.shape[longest]
        spots.append(tuple(where))
    return values.at[spots[0]].set(smallest).at[spots[1]].set(high)


def block_levels(own_key, extent, cuts, low, high):
    factor_of = 1.0
    for position, shards_of in cuts:
        heights = jax.random.uniform(jax.random.fold_in(jax.random.fold_in(own_key, 6), position), (shards_of,), jnp.float32, low / len(cuts), high / len(cuts))
        factor_of = factor_of * jnp.repeat(jnp.exp(heights), extent[position] // shards_of).reshape((-1,) + (1,) * (len(extent) - 1 - position))
    return factor_of


def noise(rng, shape, width, limit, cuts=(), kind=jnp.bfloat16):
    values = width * jax.random.normal(rng, shape, jnp.float32)
    if cuts:
        values = values * block_levels(rng, shape, cuts, -0.22, 0.18)
    return jnp.clip(values, -limit, limit).astype(kind)


def setup_inputs(seed: int = 0) -> dict:
    key_list = jax.random.split(jax.random.key(seed), 13)
    context_kv = draw_context_kv(jax.random.fold_in(key_list[12], 71), 0)
    queries = draw_queries(jax.random.fold_in(key_list[12], 71), 0)
    cont_keys = noise(key_list[2], (VARIANTS, CONT, D), 2.4, 6.0, ((0, 128), (2, 4)))
    hyena_inputs = noise(key_list[3], (3, VARIANTS, CONT, D), 1.0, 6.0, ((1, 128), (3, 4)))
    hyena_state = noise(key_list[4], (FLEN, D), 1.0, 6.0, ((0, 128), (1, 4)))
    hyena_filter = draw_hyena_filter(jax.random.fold_in(key_list[12], 71), 0)
    filter_skip = noise(key_list[6], (D,), 0.5, 3.0, ((0, 4),), jnp.float32)
    unembed = draw_unembed(jax.random.fold_in(key_list[12], 71), 0)
    ref_bases = place_ends(jax.random.randint(key_list[8], (CONT,), 0, 4), jax.random.fold_in(key_list[8], 1), 0, 3).astype(jnp.int32)
    variant_pos = place_ends(jax.random.randint(key_list[9], (VARIANTS,), 0, CONT), jax.random.fold_in(key_list[9], 1), 0, CONT - 1).astype(jnp.int32)
    allele_ids = place_ends(jax.random.randint(key_list[10], (VARIANTS,), 0, 4), jax.random.fold_in(key_list[10], 1), 0, 3).astype(jnp.int32)
    cont_lengths = draw_cont_lengths(jax.random.fold_in(key_list[12], 71), 0)
    return dict(context_kv=context_kv, queries=queries, cont_keys=cont_keys, hyena_inputs=hyena_inputs, hyena_state=hyena_state, hyena_filter=hyena_filter, filter_skip=filter_skip, unembed=unembed, ref_bases=ref_bases, variant_pos=variant_pos, allele_ids=allele_ids, cont_lengths=cont_lengths)


BASE_TOKENS = (65, 67, 71, 84)


def reference(context_kv, queries, cont_keys, hyena_inputs, hyena_state, hyena_filter, filter_skip, unembed, ref_bases, variant_pos, allele_ids, cont_lengths):
    score_scale = HEAD_DIM ** -0.5
    highest = lax.Precision.HIGHEST
    ctx_keys = context_kv[0].astype(jnp.float32).reshape(N_CTX, CTX_DEV, HEADS, HEAD_DIM)
    ctx_values = context_kv[1].astype(jnp.float32).reshape(N_CTX, CTX_DEV, HEADS, HEAD_DIM)
    out_table = unembed.astype(jnp.float32)
    window_index = (FLEN + jnp.arange(CONT)[:, None] - jnp.arange(1, FLEN + 1)[None, :]).astype(jnp.int32)
    places = jnp.arange(CONT)
    causal = places[:, None] >= places[None, :]

    def one_variant(packed):
        query_row, key_row, mixer_rows = packed
        product = (mixer_rows[1].astype(jnp.float32) * mixer_rows[2].astype(jnp.float32)).astype(jnp.bfloat16)
        sequence = jnp.concatenate([hyena_state, product], 0).astype(jnp.float32)
        windows = sequence[window_index]
        mixed = jnp.einsum('tjd,dj->td', windows, hyena_filter, precision=highest) + filter_skip[None, :] * product.astype(jnp.float32)
        hyena_row = (mixer_rows[0].astype(jnp.float32) * mixed).astype(jnp.bfloat16)
        query_heads = query_row.astype(jnp.float32).reshape(CONT, HEADS, HEAD_DIM)
        scores = jnp.einsum('thd,bkhd->bthk', query_heads, ctx_keys, precision=highest) * score_scale
        block_max = scores.max(-1)
        weights = jnp.exp(scores - block_max[..., None])
        block_total = weights.sum(-1)
        rounded = lax.optimization_barrier(weights.astype(jnp.bfloat16)).astype(jnp.float32)
        block_numer = jnp.einsum('bthk,bkhd->bthd', rounded, ctx_values, precision=highest).astype(jnp.bfloat16)
        key_heads = key_row.astype(jnp.float32).reshape(CONT, HEADS, HEAD_DIM)
        self_scores = jnp.einsum('thd,shd->ths', query_heads, key_heads, precision=highest) * score_scale
        self_scores = jnp.where(causal[:, None, :], self_scores, -jnp.inf)
        self_max = self_scores.max(-1)
        self_weight = jnp.exp(self_scores - self_max[..., None])
        self_total = self_weight.sum(-1)
        self_rounded = lax.optimization_barrier(self_weight.astype(jnp.bfloat16)).astype(jnp.float32)
        value_heads = hyena_row.astype(jnp.float32).reshape(CONT, HEADS, HEAD_DIM)
        self_numer = jnp.einsum('ths,shd->thd', self_rounded, value_heads, precision=highest).astype(jnp.bfloat16)
        row_peak = jnp.maximum(block_max.max(0), self_max)
        block_scale = jnp.exp(block_max - row_peak[None])
        self_scale = jnp.exp(self_max - row_peak)
        denominator = (block_scale * block_total).sum(0) + self_scale * self_total
        attended = (block_numer.astype(jnp.float32) * (block_scale / denominator[None])[..., None]).sum(0)
        attended = attended + self_numer.astype(jnp.float32) * (self_scale / denominator)[..., None]
        logits = jnp.dot(attended.reshape(CONT, D), out_table, precision=highest)
        return hyena_row, logits

    hyena_out, logits = lax.map(one_variant, (queries, cont_keys, jnp.moveaxis(hyena_inputs, 1, 0)))
    peak = logits.max(-1, keepdims=True)
    log_total = peak[..., 0] + jnp.log(jnp.exp(logits - peak).sum(-1))
    codes = jnp.where(places[None, :] == variant_pos[:, None], allele_ids[:, None], ref_bases[None, :]).astype(jnp.int32)
    base_ids = jnp.array(BASE_TOKENS, jnp.int32)
    targets = base_ids[codes].astype(jnp.int32)
    picked = jnp.take_along_axis(logits, targets[..., None], -1)[..., 0]
    log_probs = picked - log_total
    variant_scores = jnp.where(places[None, :] < cont_lengths[:, None], log_probs, 0.0).sum(-1)
    return hyena_out, log_probs, variant_scores
```

```python
import functools
import math

import jax
import jax.numpy as jnp
from jax import lax
from jax.experimental import pallas as pl
from jax.experimental.pallas import tpu as pltpu
from jax.sharding import PartitionSpec as P

HEAD_DIM = 128
BASE_TOKENS = (65, 67, 71, 84)
EXP_SCALE = HEAD_DIM ** (-0.5) * math.log2(math.e)
LOWEST = -3.0e38
BF16 = jnp.bfloat16
F32 = jnp.float32


def spread_kernel(
    n,
    tp_count,
    kv_ref,
    q_ref,
    ck_ref,
    hy_ref,
    state_ref,
    filt_ref,
    skip_ref,
    unembed_ref,
    bases_ref,
    pos_ref,
    allele_ref,
    length_ref,
    hyena_ref,
    log_probs_ref,
    score_ref,
    q_own,
    kv_own,
    state_src,
    state_all,
    state_rows,
    gather_r,
    gather_l,
    gather_far,
    part_out_r,
    part_out_l,
    part_far,
    stat_out_r,
    stat_out_l,
    stat_far,
    part_in_r,
    part_in_l,
    stat_in_r,
    stat_in_l,
    values_t,
    merged,
    merged_stat,
    back,
    back_stat,
    state_part,
    state_parts,
    stat_square,
    logit_parts,
    targets,
    padded,
    mixed,
    taps_own,
    q_v,
    ck_v,
    hy_v,
    filt_v,
    unembed_v,
    local_sem,
    spread_send,
    spread_recv,
    gather_send_r,
    gather_recv_r,
    gather_send_l,
    gather_recv_l,
    part_send,
    part_recv_r,
    part_recv_l,
    stat_send,
    stat_recv_r,
    stat_recv_l,
    back_send,
    back_recv,
    tp_send,
    tp_recv,
):
    half = n // 2
    heads = 2 * n
    positions = q_v.shape[0]
    rows = heads * positions
    taps = filt_v.shape[1]
    channels = heads * HEAD_DIM
    vocab = unembed_v.shape[1]

    ctx = lax.axis_index("ctx")
    var = lax.axis_index("var")
    tp = lax.axis_index("tp")
    z = lax.div(ctx, 4)
    core = lax.rem(ctx, 2)
    y = var * 2 + lax.div(lax.rem(ctx, 4), 2)
    ring = (1 - core) * z + core * y
    other = (1 - core) * y + core * z
    head = (1 - core) * y + core * (n + z)

    def device(z_to, y_to, core_to):
        return {"ctx": z_to * 4 + lax.rem(y_to, 2) * 2 + core_to, "var": lax.div(y_to, 2)}

    def ring_device(offset):
        return device(
            lax.rem(z + offset * (1 - core), n), lax.rem(y + offset * core, n), core
        )

    def remote(src, dst, send_sem, recv_sem, device_id):
        return pltpu.make_async_remote_copy(
            src_ref=src,
            dst_ref=dst,
            send_sem=send_sem,
            recv_sem=recv_sem,
            device_id=device_id,
            device_id_type=pl.DeviceIdType.MESH,
        )

    def wait_for(ref, sem):
        pltpu.make_async_copy(ref, ref, sem).wait()

    def lanes_of(h):
        return pl.ds(pl.multiple_of(h * HEAD_DIM, HEAD_DIM), HEAD_DIM)

    loads = [
        pltpu.make_async_copy(hy_ref.at[:, 0], hy_v, local_sem.at[0]),
        pltpu.make_async_copy(filt_ref, filt_v, local_sem.at[1]),
        pltpu.make_async_copy(q_ref.at[0], q_v, local_sem.at[2]),
        pltpu.make_async_copy(ck_ref.at[0], ck_v, local_sem.at[3]),
        pltpu.make_async_copy(unembed_ref, unembed_v, local_sem.at[4]),
    ]
    for load in loads:
        load.start()

    cut = rows // 2
    part_in_r[half - 1, :, cut:] = jnp.zeros((HEAD_DIM, cut), BF16)
    part_in_l[half - 1, :, :cut] = jnp.zeros((HEAD_DIM, cut), BF16)
    stat_in_r[half - 1, 0:1, cut:] = jnp.full((1, cut), LOWEST, F32)
    stat_in_l[half - 1, 0:1, :cut] = jnp.full((1, cut), LOWEST, F32)
    stat_in_r[half - 1, 1:2, cut:] = jnp.zeros((1, cut), F32)
    stat_in_l[half - 1, 1:2, :cut] = jnp.zeros((1, cut), F32)
    for h in range(heads):
        state_src[h] = state_ref[:, h * HEAD_DIM : (h + 1) * HEAD_DIM].astype(F32)

    barrier = pltpu.get_barrier_semaphore()

    def greet(device_id):
        pl.semaphore_signal(
            barrier, inc=1, device_id=device_id, device_id_type=pl.DeviceIdType.MESH
        )

    def greet_offset(k, carry):
        for c_to in range(2):
            greet(device(z, lax.rem(y + k, n), c_to))
            greet(device(lax.rem(z + k, n), y, c_to))
        return carry

    lax.fori_loop(1, n, greet_offset, 0)
    greet(device(z, y, 1 - core))
    for k in range(1, tp_count):
        greet({"tp": lax.rem(tp + k, tp_count)})
    pl.semaphore_wait(barrier, 4 * (n - 1) + 1 + tp_count - 1)

    slot_y = 2 * y + core
    slot_z = 2 * z + core
    slot_self = 2 * other + core
    slot_sibling = 2 * ring + core
    head_sibling = (1 - core) * (n + z) + core * y
    sibling = device(z, y, 1 - core)

    def q_copy(h, slot, device_id):
        return remote(
            q_ref.at[0, :, lanes_of(h)],
            q_own.at[slot],
            spread_send.at[0],
            spread_recv.at[0],
            device_id,
        )

    def state_copy(h, ring_to, slot, device_id):
        return remote(
            state_src.at[h],
            state_all.at[ring_to, slot],
            spread_send.at[1],
            spread_recv.at[1],
            device_id,
        )

    def kv_copy(h, slot, device_id):
        return remote(
            kv_ref.at[:, :, lanes_of(h)],
            kv_own.at[slot],
            spread_send.at[2],
            spread_recv.at[2],
            device_id,
        )

    def send_q(k, carry):
        y_to = lax.rem(y + k, n)
        z_to = lax.rem(z + k, n)
        q_copy(y_to, slot_y, device(z, y_to, 0)).start()
        q_copy(n + z_to, slot_z, device(z_to, y, 1)).start()
        state_copy(y_to, z, slot_y, device(z, y_to, 0)).start()
        state_copy(n + z_to, y, slot_z, device(z_to, y, 1)).start()
        return carry

    def send_kv(k, carry):
        y_to = lax.rem(y + k, n)
        z_to = lax.rem(z + k, n)
        kv_copy(y_to, slot_y, device(z, y_to, 0)).start()
        kv_copy(n + z_to, slot_z, device(z_to, y, 1)).start()
        return carry

    self_q = pltpu.make_async_copy(
        q_ref.at[0, :, lanes_of(head)], q_own.at[slot_self], local_sem.at[5]
    )
    self_kv = pltpu.make_async_copy(
        kv_ref.at[:, :, lanes_of(head)], kv_own.at[slot_self], local_sem.at[6]
    )
    self_state = pltpu.make_async_copy(
        state_src.at[head], state_all.at[ring, slot_self], local_sem.at[7]
    )
    lax.fori_loop(1, n, send_q, 0)
    q_copy(head_sibling, slot_sibling, sibling).start()
    state_copy(head_sibling, other, slot_sibling, sibling).start()
    self_q.start()
    self_state.start()
    lax.fori_loop(1, n, send_kv, 0)
    kv_copy(head_sibling, slot_sibling, sibling).start()
    self_kv.start()

    loads[0].wait()
    product = (hy_v[1].astype(F32) * hy_v[2].astype(F32)).astype(BF16).astype(F32)
    padded[0:positions, :] = jnp.zeros((positions, channels), F32)
    padded[positions:, :] = product
    mixed[...] = skip_ref[...] * product
    row_index = lax.broadcasted_iota(jnp.int32, (positions, vocab), 0)
    codes = jnp.zeros((positions, vocab), jnp.int32)
    for t in range(positions):
        codes = jnp.where(row_index == t, bases_ref[t], codes)
    codes = jnp.where(row_index == pos_ref[0], allele_ref[0], codes)
    wanted = jnp.zeros((positions, vocab), jnp.int32)
    for code, token in enumerate(BASE_TOKENS):
        wanted = jnp.where(codes == code, token, wanted)
    targets[...] = wanted

    right = ring_device(1)
    left = ring_device(n - 1)
    part = heads // 2

    def gather_right(d, src):
        if d < half:
            return remote(
                src, gather_r.at[d - 1], gather_send_r.at[d - 1], gather_recv_r.at[d - 1], right
            )
        return remote(
            src.at[0:part],
            gather_far.at[0:part],
            gather_send_r.at[d - 1],
            gather_recv_r.at[d - 1],
            right,
        )

    def gather_left(d, src):
        if d < half:
            return remote(
                src, gather_l.at[d - 1], gather_send_l.at[d - 1], gather_recv_l.at[d - 1], left
            )
        return remote(
            src.at[part:heads],
            gather_far.at[part:heads],
            gather_send_l.at[d - 1],
            gather_recv_l.at[d - 1],
            left,
        )

    gathers = []

    def pass_on(d):
        for copy in (
            gather_right(d, q_own if d == 1 else gather_r.at[d - 2]),
            gather_left(d, q_own if d == 1 else gather_l.at[d - 2]),
        ):
            copy.start()
            gathers.append(copy)

    wait_for(q_own.at[0 : heads - 1], spread_recv.at[0])
    self_q.wait()
    pass_on(1)

    wait_for(state_all.at[0, 0 : heads - 1], spread_recv.at[1])
    self_state.wait()

    def send_state(k, carry):
        remote(
            state_all.at[ring],
            state_all.at[ring],
            spread_send.at[3],
            spread_recv.at[3],
            ring_device(k),
        ).start()
        return carry

    lax.fori_loop(1, n, send_state, 0)

    loads[1].wait()

    def own_taps(h, carry):
        lanes = lanes_of(h)
        coeffs = jnp.transpose(filt_v[lanes, :])
        total = mixed[:, lanes]
        for j in range(1, positions):
            total = total + padded[positions - j : 2 * positions - j, lanes] * coeffs[j - 1 : j, :]
        mixed[:, lanes] = total
        return carry

    lax.fori_loop(0, part, own_taps, 0)
    if half > 1:
        for copy in gathers[-2:]:
            copy.wait_recv()
        pass_on(2)
    lax.fori_loop(part, heads, own_taps, 0)
    if half > 2:
        for copy in gathers[-2:]:
            copy.wait_recv()
        pass_on(3)

    taps_own[...] = jnp.transpose(filt_v[lanes_of(head), :])
    state_rows[taps:, :] = jnp.zeros((positions, HEAD_DIM), F32)
    wait_for(state_all.at[0 : n - 1], spread_recv.at[3])

    def place_row(index, carry):
        at = lax.div(index, heads)
        slot = lax.rem(index, heads)
        spot = lax.div(slot, 2)
        z_of = (1 - core) * at + core * spot
        y_of = (1 - core) * spot + core * at
        row = (z_of * 4 + lax.rem(y_of, 2) * 2 + lax.rem(slot, 2)) * half + lax.div(y_of, 2)
        state_rows[pl.ds(row, 1), :] = state_all[at, slot]
        return carry

    lax.fori_loop(0, n * heads, place_row, 0)

    def state_taps(step, total):
        base = pl.multiple_of(step * 8, 8)
        for b in range(8):
            total = total + (
                state_rows[pl.ds(base + b, positions), :]
                * taps_own[pl.ds(taps - 1 - b - base, 1), :]
            )
        return total

    state_part[...] = lax.fori_loop(
        0, taps // 8, state_taps, jnp.zeros((positions, HEAD_DIM), F32)
    ).astype(BF16)

    def back_device(k, c_to):
        spot = lax.rem(other + k, n)
        return (
            2 * spot + c_to,
            device((1 - core) * z + core * spot, (1 - core) * spot + core * y, c_to),
        )

    def state_back(device_id):
        return remote(
            state_part, state_parts.at[head], back_send.at[0], back_recv.at[0], device_id
        )

    def send_state_back(k, carry):
        for c_to in range(2):
            state_back(back_device(k, c_to)[1]).start()
        return carry

    lax.fori_loop(1, n, send_state_back, 0)
    state_back(sibling).start()
    state_parts[head] = state_part[...]

    if half > 3:
        for d in range(4, half + 1):
            for copy in gathers[-2:]:
                copy.wait_recv()
            pass_on(d)

    wait_for(kv_own.at[0 : heads - 1], spread_recv.at[2])
    self_kv.wait()
    context = heads * kv_own.shape[2]
    values_t[...] = jnp.transpose(kv_own[:, 1].reshape(context, HEAD_DIM))

    def attend(chunk):
        keys = kv_own[:, 0].reshape(context, HEAD_DIM)
        numer, peak, total = [], [], []
        width = min(256, rows)
        for first in range(0, rows, width):
            block = chunk[first : first + width]
            scores = lax.dot_general(
                keys, block, (((1,), (1,)), ((), ())), preferred_element_type=F32
            )
            top = jnp.max(scores, 0, keepdims=True)
            weights = jnp.exp2((scores - top) * EXP_SCALE)
            peak.append(top)
            total.append(jnp.sum(weights, 0, keepdims=True))
            numer.append(
                jnp.dot(values_t[...], weights.astype(BF16), preferred_element_type=F32)
            )
        return (
            jnp.concatenate(numer, 1),
            jnp.concatenate(peak, 1),
            jnp.concatenate(total, 1),
        )

    def merge(a, b):
        peak = jnp.maximum(a[1], b[1])
        scale_a = jnp.exp2((a[1] - peak) * EXP_SCALE)
        scale_b = jnp.exp2((b[1] - peak) * EXP_SCALE)
        return (a[0] * scale_a + b[0] * scale_b, peak, a[2] * scale_a + b[2] * scale_b)

    def arrived(part_in, stat_in, s):
        return (part_in[s].astype(F32), stat_in[s, 0:1, :], stat_in[s, 1:2, :])

    for copy in gathers[-2:]:
        copy.wait_recv()
    far = attend(gather_far[...].reshape(rows, HEAD_DIM))
    part_far[...] = far[0].astype(BF16)
    stat_far[0:1, :] = far[1]
    stat_far[1:2, :] = far[2]
    far_copies = []
    for side, part_in, stat_in, part_recv, stat_recv, device_id in (
        (0, part_in_r, stat_in_r, part_recv_r, stat_recv_r, right),
        (1, part_in_l, stat_in_l, part_recv_l, stat_recv_l, left),
    ):
        span = pl.ds(side * cut, cut)
        far_copies.append(
            remote(
                part_far.at[:, span],
                part_in.at[half - 1, :, span],
                part_send.at[side, half - 1],
                part_recv.at[half - 1],
                device_id,
            )
        )
        far_copies.append(
            remote(
                stat_far.at[:, span],
                stat_in.at[half - 1, :, span],
                stat_send.at[side, half - 1],
                stat_recv.at[half - 1],
                device_id,
            )
        )
    for copy in far_copies:
        copy.start()

    wait_for(state_parts.at[0 : heads - 1], back_recv.at[0])
    for h in range(heads):
        lanes = slice(h * HEAD_DIM, (h + 1) * HEAD_DIM)
        hyena_ref[0, :, lanes] = (
            hy_v[0, :, lanes].astype(F32) * (mixed[:, lanes] + state_parts[h].astype(F32))
        ).astype(BF16)
    loads[2].wait()
    loads[3].wait()
    group = HEAD_DIM // positions
    own = []
    row_at = lax.broadcasted_iota(jnp.int32, (HEAD_DIM, HEAD_DIM), 0)
    col_at = lax.broadcasted_iota(jnp.int32, (HEAD_DIM, HEAD_DIM), 1)
    seen = (lax.div(row_at, positions) == lax.div(col_at, positions)) & (col_at <= row_at)

    def stacked(ref, g):
        return jnp.concatenate(
            [ref[:, h * HEAD_DIM : (h + 1) * HEAD_DIM] for h in range(g * group, (g + 1) * group)],
            0,
        )

    for g in range(heads // group):
        scores = lax.dot_general(
            stacked(q_v, g), stacked(ck_v, g), (((1,), (1,)), ((), ())), preferred_element_type=F32
        )
        scores = jnp.where(seen, scores, LOWEST)
        top = jnp.max(scores, 1, keepdims=True)
        weights = jnp.where(seen, jnp.exp2((scores - top) * EXP_SCALE), 0.0)
        total = jnp.sum(weights, 1, keepdims=True)
        numer = jnp.dot(
            weights.astype(BF16), stacked(hyena_ref.at[0], g), preferred_element_type=F32
        )
        own.append((numer, top, total))

    def part_copy(s, side):
        part_out, part_in, part_recv, device_id = (
            (part_out_r, part_in_r, part_recv_r, right),
            (part_out_l, part_in_l, part_recv_l, left),
        )[side]
        return remote(
            part_out.at[s],
            part_in.at[s - 1],
            part_send.at[side, s - 1],
            part_recv.at[s - 1],
            device_id,
        )

    def stat_copy(s, side):
        stat_out, stat_in, stat_recv, device_id = (
            (stat_out_r, stat_in_r, stat_recv_r, right),
            (stat_out_l, stat_in_l, stat_recv_l, left),
        )[side]
        return remote(
            stat_out.at[s],
            stat_in.at[s - 1],
            stat_send.at[side, s - 1],
            stat_recv.at[s - 1],
            device_id,
        )

    def wait_part(s, side, span):
        part_in, part_recv, stat_in, stat_recv = (
            (part_in_r, part_recv_r, stat_in_r, stat_recv_r),
            (part_in_l, part_recv_l, stat_in_l, stat_recv_l),
        )[side]
        wait_for(part_in.at[s, :, span], part_recv.at[s])
        wait_for(stat_in.at[s, :, span], stat_recv.at[s])

    def reduce_step(s, span_r, span_l):
        for side, gathered, part_in, stat_in, part_out, stat_out, span in (
            (0, gather_l, part_in_r, stat_in_r, part_out_r, stat_out_r, span_r),
            (1, gather_r, part_in_l, stat_in_l, part_out_l, stat_out_l, span_l),
        ):
            mine = attend(gathered[s - 1].reshape(rows, HEAD_DIM))
            wait_part(s, side, span)
            numer, peak, total = merge(mine, arrived(part_in, stat_in, s))
            part_out[s] = numer.astype(BF16)
            stat_out[s, 0:1, :] = peak
            stat_out[s, 1:2, :] = total
            part_copy(s, side).start()
            stat_copy(s, side).start()

    whole = pl.ds(0, rows)
    first_r, first_l = pl.ds(0, cut), pl.ds(cut, cut)
    if half > 1:
        reduce_step(half - 1, first_r, first_l)

    def reduce_more(index, carry):
        reduce_step(half - 2 - index, whole, whole)
        return carry

    if half > 2:
        lax.fori_loop(0, half - 2, reduce_more, 0)

    mine = attend(q_own[...].reshape(rows, HEAD_DIM))
    wait_part(0, 0, whole if half > 1 else first_r)
    mine = merge(mine, arrived(part_in_r, stat_in_r, 0))
    wait_part(0, 1, whole if half > 1 else first_l)
    numer, peak, total = merge(mine, arrived(part_in_l, stat_in_l, 0))
    merged[...] = jnp.transpose(numer).astype(BF16).reshape(merged.shape)
    for b in range(rows // HEAD_DIM):
        merged_stat[b, 0:1, :] = peak[:, b * HEAD_DIM : (b + 1) * HEAD_DIM]
        merged_stat[b, 1:2, :] = total[:, b * HEAD_DIM : (b + 1) * HEAD_DIM]

    def back_copy(slot, device_id):
        return remote(
            merged.at[slot], back.at[head], back_send.at[1], back_recv.at[1], device_id
        )

    def back_stat_copy(slot, device_id):
        return remote(
            merged_stat.at[lax.div(slot, group)],
            back_stat.at[head],
            back_send.at[2],
            back_recv.at[2],
            device_id,
        )

    def send_back(k, carry):
        for c_to in range(2):
            slot, device_id = back_device(k, c_to)
            back_copy(slot, device_id).start()
            back_stat_copy(slot, device_id).start()
        return carry

    lax.fori_loop(1, n, send_back, 0)
    slot_other = 2 * other + 1 - core
    back_copy(slot_other, sibling).start()
    back_stat_copy(slot_other, sibling).start()
    back[head] = merged[slot_self]
    back_stat[head] = merged_stat[lax.div(slot_self, group)]

    loads[4].wait()
    stat_square[...] = jnp.zeros_like(stat_square)
    wait_for(back_stat.at[0 : heads - 1], back_recv.at[2])
    for first, slot in ((0, slot_y), (n, slot_z)):
        shift = lax.rem(HEAD_DIM - lax.rem(slot, group) * positions, HEAD_DIM)
        for kind in range(2):
            stat_square[kind * heads + first : kind * heads + first + n, :] = pltpu.roll(
                back_stat[first : first + n, kind, :], shift, 1
            )
    columns = jnp.transpose(stat_square[...])
    wait_for(back.at[0 : heads - 1], back_recv.at[1])
    pieces = []
    for g in range(heads // group):
        chosen = range(g * group, (g + 1) * group)
        peak = jnp.concatenate([columns[0:positions, h : h + 1] for h in chosen], 0)
        total = jnp.concatenate(
            [columns[0:positions, heads + h : heads + h + 1] for h in chosen], 0
        )
        numer = back[g * group : (g + 1) * group].reshape(HEAD_DIM, HEAD_DIM).astype(F32)
        numer, _, total = merge((numer, peak, total), own[g])
        attended = numer / total
        pieces += [attended[i * positions : (i + 1) * positions] for i in range(group)]
    attended = jnp.concatenate(pieces, 1)
    high = attended.astype(BF16)
    low = (attended - high.astype(F32)).astype(BF16)
    both = jnp.dot(
        jnp.concatenate([high, low], 0), unembed_v[...], preferred_element_type=F32
    )
    logit_parts[tp] = both[0:positions] + both[positions:]

    tp_copies = [
        remote(
            logit_parts.at[tp],
            logit_parts.at[tp],
            tp_send,
            tp_recv,
            {"tp": lax.rem(tp + k, tp_count)},
        )
        for k in range(1, tp_count)
    ]
    for copy in tp_copies:
        copy.start()
    if tp_count > 1:
        wait_for(logit_parts.at[0 : tp_count - 1], tp_recv)
    logits = logit_parts[0]
    for k in range(1, tp_count):
        logits = logits + logit_parts[k]
    top = jnp.max(logits, 1, keepdims=True)
    log_total = top + jnp.log(jnp.sum(jnp.exp(logits - top), 1, keepdims=True))
    vocab_at = lax.broadcasted_iota(jnp.int32, (positions, vocab), 1)
    picked = jnp.sum(jnp.where(vocab_at == targets[...], logits, 0.0), 1, keepdims=True)
    log_probs = picked - log_total
    place = lax.broadcasted_iota(jnp.int32, (positions, positions), 0)
    lane = lax.broadcasted_iota(jnp.int32, (positions, positions), 1)
    log_row = jnp.sum(jnp.where(place == lane, log_probs, 0.0), 0, keepdims=True)
    log_probs_ref[...] = log_row
    lane_row = lax.broadcasted_iota(jnp.int32, (1, positions), 1)
    score_ref[...] = jnp.sum(
        jnp.where(lane_row < length_ref[0], log_row, 0.0), 1, keepdims=True
    )

    wait_for(q_own.at[0 : heads - 1], spread_send.at[0])
    wait_for(state_all.at[0, 0 : heads - 1], spread_send.at[1])
    wait_for(kv_own.at[0 : heads - 1], spread_send.at[2])
    wait_for(state_all.at[0 : n - 1], spread_send.at[3])
    for copy in gathers + far_copies:
        copy.wait_send()
    for s in range(1, half):
        for side in range(2):
            part_copy(s, side).wait_send()
            stat_copy(s, side).wait_send()
    wait_for(state_parts.at[0 : heads - 1], back_send.at[0])
    wait_for(back.at[0 : heads - 1], back_send.at[1])
    wait_for(back_stat.at[0 : heads - 1], back_send.at[2])
    if tp_count > 1:
        wait_for(logit_parts.at[0 : tp_count - 1], tp_send)


def on_device(
    n,
    tp_count,
    context_kv,
    queries,
    cont_keys,
    hyena_inputs,
    hyena_state,
    hyena_filter,
    filter_skip,
    unembed,
    ref_bases,
    variant_pos,
    allele_ids,
    cont_lengths,
):
    positions, channels = queries.shape[1:]
    block = context_kv.shape[1]
    taps = hyena_filter.shape[1]
    vocab = unembed.shape[1]
    heads = channels // HEAD_DIM
    half = n // 2
    rows = heads * positions
    steps = max(1, half - 1)
    vmem = pltpu.VMEM
    dma = pltpu.SemaphoreType.DMA
    scratch = [
        vmem((heads, positions, HEAD_DIM), BF16),
        vmem((heads, 2, block, HEAD_DIM), BF16),
        vmem((heads, 1, HEAD_DIM), F32),
        vmem((n, heads, 1, HEAD_DIM), F32),
        vmem((taps + positions, HEAD_DIM), F32),
        vmem((steps, heads, positions, HEAD_DIM), BF16),
        vmem((steps, heads, positions, HEAD_DIM), BF16),
        vmem((heads, positions, HEAD_DIM), BF16),
        vmem((half, HEAD_DIM, rows), BF16),
        vmem((half, HEAD_DIM, rows), BF16),
        vmem((HEAD_DIM, rows), BF16),
        vmem((half, 2, rows), F32),
        vmem((half, 2, rows), F32),
        vmem((2, rows), F32),
        vmem((half, HEAD_DIM, rows), BF16),
        vmem((half, HEAD_DIM, rows), BF16),
        vmem((half, 2, rows), F32),
        vmem((half, 2, rows), F32),
        vmem((HEAD_DIM, heads * block), BF16),
        vmem((heads, positions, HEAD_DIM), BF16),
        vmem((rows // HEAD_DIM, 2, HEAD_DIM), F32),
        vmem((heads, positions, HEAD_DIM), BF16),
        vmem((heads, 2, HEAD_DIM), F32),
        vmem((positions, HEAD_DIM), BF16),
        vmem((heads, positions, HEAD_DIM), BF16),
        vmem((HEAD_DIM, HEAD_DIM), F32),
        vmem((tp_count, positions, vocab), F32),
        vmem((positions, vocab), jnp.int32),
        vmem((2 * positions, channels), F32),
        vmem((positions, channels), F32),
        vmem((taps, HEAD_DIM), F32),
        vmem((positions, channels), BF16),
        vmem((positions, channels), BF16),
        vmem((3, positions, channels), BF16),
        vmem((channels, taps), F32),
        vmem((channels, vocab), BF16),
        dma((8,)),
        dma((4,)),
        dma((4,)),
        dma((half,)),
        dma((half,)),
        dma((half,)),
        dma((half,)),
        dma((2, half)),
        dma((half,)),
        dma((half,)),
        dma((2, half)),
        dma((half,)),
        dma((half,)),
        dma((3,)),
        dma((3,)),
        dma,
        dma,
    ]
    hbm = pl.BlockSpec(memory_space=pl.ANY)
    in_vmem = pl.BlockSpec(memory_space=pltpu.VMEM)
    in_smem = pl.BlockSpec(memory_space=pltpu.SMEM)
    hyena_out, log_probs, score = pl.pallas_call(
        functools.partial(spread_kernel, n, tp_count),
        out_shape=(
            jax.ShapeDtypeStruct((1, positions, channels), BF16),
            jax.ShapeDtypeStruct((1, positions), F32),
            jax.ShapeDtypeStruct((1, 1), F32),
        ),
        in_specs=[hbm] * 4 + [in_vmem, hbm, in_vmem, hbm] + [in_smem] * 4,
        out_specs=(in_vmem, in_vmem, in_vmem),
        scratch_shapes=scratch,
        compiler_params=pltpu.CompilerParams(
            collective_id=0, has_side_effects=True, vmem_limit_bytes=48 * 1024 * 1024
        ),
    )(
        context_kv,
        queries,
        cont_keys,
        hyena_inputs,
        hyena_state,
        hyena_filter,
        filter_skip.reshape(1, channels),
        unembed,
        ref_bases,
        variant_pos,
        allele_ids,
        cont_lengths,
    )
    return hyena_out, log_probs, score.reshape(1)


def solution(mesh):
    n = mesh.shape["ctx"] // 4
    placed = (
        P(None, ("ctx", "var"), "tp"),
        P(("ctx", "var"), None, "tp"),
        P(("ctx", "var"), None, "tp"),
        P(None, ("ctx", "var"), None, "tp"),
        P(("ctx", "var"), "tp"),
        P("tp", None),
        P("tp"),
        P("tp", None),
        P(),
        P(("ctx", "var")),
        P(("ctx", "var")),
        P(("ctx", "var")),
    )
    return jax.shard_map(
        functools.partial(on_device, n, mesh.shape["tp"]),
        mesh=mesh,
        in_specs=placed,
        out_specs=(P(("ctx", "var"), None, "tp"), P(("ctx", "var"), None), P(("ctx", "var"))),
        check_vma=False,
    )
```

```python
import functools
import math

import jax
import jax.numpy as jnp
from jax import lax
from jax.experimental import pallas as pl
from jax.experimental.pallas import tpu as pltpu
from jax.sharding import PartitionSpec as P

HEAD_DIM = 128
BASE_TOKENS = (65, 67, 71, 84)
EXP_SCALE = HEAD_DIM ** (-0.5) * math.log2(math.e)
LOWEST = -3.0e38
BF16 = jnp.bfloat16
F32 = jnp.float32


def spread_kernel(
    n,
    tp_count,
    kv_ref,
    q_ref,
    ck_ref,
    hy_ref,
    state_ref,
    filt_ref,
    skip_ref,
    unembed_ref,
    bases_ref,
    pos_ref,
    allele_ref,
    length_ref,
    hyena_ref,
    log_probs_ref,
    score_ref,
    q_own,
    keys,
    values_own,
    values_t,
    state_src,
    state_all,
    state_rows,
    gathered,
    part_out,
    stat_out,
    part_in,
    stat_in,
    sum_numer,
    sum_stat,
    merged,
    merged_stat,
    back,
    back_stat,
    state_part,
    state_parts,
    stat_square,
    logit_parts,
    targets,
    padded,
    mixed,
    taps_own,
    q_v,
    kv_v,
    ck_v,
    hy_v,
    filt_v,
    unembed_v,
    state_v,
    skip_v,
    bases_s,
    pos_s,
    allele_s,
    length_s,
    local_sem,
    spread_send,
    spread_recv,
    gather_send,
    gather_recv,
    part_send,
    part_recv,
    stat_send,
    stat_recv,
    keys_send,
    keys_recv,
    values_send,
    values_recv,
    back_send,
    back_recv,
    tp_send,
    tp_recv,
):
    heads = 2 * n
    positions = q_v.shape[0]
    rows = heads * positions
    taps = filt_v.shape[1]
    channels = heads * HEAD_DIM
    vocab = unembed_v.shape[1]

    ctx = lax.axis_index("ctx")
    var = lax.axis_index("var")
    tp = lax.axis_index("tp")
    z = lax.div(ctx, 4)
    core = lax.rem(ctx, 2)
    y = var * 2 + lax.div(lax.rem(ctx, 4), 2)
    ring = (1 - core) * z + core * y
    other = (1 - core) * y + core * z
    head = (1 - core) * y + core * (n + z)

    def device(z_to, y_to, core_to):
        return {"ctx": z_to * 4 + lax.rem(y_to, 2) * 2 + core_to, "var": lax.div(y_to, 2)}

    def ring_device(offset):
        return device(
            lax.rem(z + offset * (1 - core), n), lax.rem(y + offset * core, n), core
        )

    sibling = device(z, y, 1 - core)

    def remote(src, dst, send_sem, recv_sem, device_id):
        return pltpu.make_async_remote_copy(
            src_ref=src,
            dst_ref=dst,
            send_sem=send_sem,
            recv_sem=recv_sem,
            device_id=device_id,
            device_id_type=pl.DeviceIdType.MESH,
        )

    def wait_for(ref, sem):
        pltpu.make_async_copy(ref, ref, sem).wait()

    def lanes_of(h):
        return pl.ds(pl.multiple_of(h * HEAD_DIM, HEAD_DIM), HEAD_DIM)

    barrier = pltpu.get_barrier_semaphore()

    def greet(device_id):
        pl.semaphore_signal(
            barrier, inc=1, device_id=device_id, device_id_type=pl.DeviceIdType.MESH
        )

    def greet_offset(k, carry):
        for core_to in range(2):
            greet(device(z, lax.rem(y + k, n), core_to))
            greet(device(lax.rem(z + k, n), y, core_to))
        return carry

    lax.fori_loop(1, n, greet_offset, 0)
    greet(sibling)
    for k in range(1, tp_count):
        greet({"tp": lax.rem(tp + k, tp_count)})

    small = [
        pltpu.make_async_copy(src, dst, local_sem.at[8 + i])
        for i, (src, dst) in enumerate(
            (
                (state_ref, state_v),
                (skip_ref, skip_v),
                (bases_ref, bases_s),
                (pos_ref, pos_s),
                (allele_ref, allele_s),
                (length_ref, length_s),
            )
        )
    ]
    for load in small:
        load.start()
    load_q = pltpu.make_async_copy(q_ref.at[0], q_v, local_sem.at[2])
    load_kv = pltpu.make_async_copy(kv_ref, kv_v, local_sem.at[14])
    load_hyena = pltpu.make_async_copy(hy_ref.at[:, 0], hy_v, local_sem.at[0])
    load_filter = pltpu.make_async_copy(filt_ref, filt_v, local_sem.at[1])
    load_keys = pltpu.make_async_copy(ck_ref.at[0], ck_v, local_sem.at[3])
    load_unembed = pltpu.make_async_copy(unembed_ref, unembed_v, local_sem.at[4])
    for load in (load_q, load_kv, load_hyena, load_filter, load_keys, load_unembed):
        load.start()

    small[0].wait()
    for h in range(heads):
        state_src[h] = state_v[:, h * HEAD_DIM : (h + 1) * HEAD_DIM].astype(F32)
    load_q.wait()
    load_kv.wait()
    pl.semaphore_wait(barrier, 4 * (n - 1) + 1 + tp_count - 1)

    slot_y = 2 * y + core
    slot_z = 2 * z + core
    slot_self = 2 * other + core
    slot_sibling = 2 * ring + core
    head_sibling = (1 - core) * (n + z) + core * y

    def q_copy(h, slot, device_id):
        return remote(
            q_v.at[:, lanes_of(h)],
            q_own.at[slot],
            spread_send.at[0],
            spread_recv.at[0],
            device_id,
        )

    def state_copy(h, ring_to, slot, device_id):
        return remote(
            state_src.at[h],
            state_all.at[ring_to, slot],
            spread_send.at[1],
            spread_recv.at[1],
            device_id,
        )

    def keys_copy(h, slot, device_id):
        return remote(
            kv_v.at[0, :, lanes_of(h)],
            keys.at[1, slot],
            spread_send.at[2],
            spread_recv.at[2],
            device_id,
        )

    def values_copy(h, slot, device_id):
        return remote(
            kv_v.at[1, :, lanes_of(h)],
            values_own.at[slot],
            spread_send.at[4],
            spread_recv.at[4],
            device_id,
        )

    def send_all(copy):
        def send(k, carry):
            y_to = lax.rem(y + k, n)
            z_to = lax.rem(z + k, n)
            copy(y_to, slot_y, device(z, y_to, 0)).start()
            copy(n + z_to, slot_z, device(z_to, y, 1)).start()
            return carry

        lax.fori_loop(1, n, send, 0)
        copy(head_sibling, slot_sibling, sibling).start()

    def send_state(k, carry):
        y_to = lax.rem(y + k, n)
        z_to = lax.rem(z + k, n)
        state_copy(y_to, z, slot_y, device(z, y_to, 0)).start()
        state_copy(n + z_to, y, slot_z, device(z_to, y, 1)).start()
        return carry

    self_q = pltpu.make_async_copy(
        q_v.at[:, lanes_of(head)], q_own.at[slot_self], local_sem.at[5]
    )
    self_keys = pltpu.make_async_copy(
        kv_v.at[0, :, lanes_of(head)], keys.at[1, slot_self], local_sem.at[6]
    )
    self_values = pltpu.make_async_copy(
        kv_v.at[1, :, lanes_of(head)], values_own.at[slot_self], local_sem.at[15]
    )
    self_state = pltpu.make_async_copy(
        state_src.at[head], state_all.at[ring, slot_self], local_sem.at[7]
    )
    send_all(q_copy)
    self_q.start()
    lax.fori_loop(1, n, send_state, 0)
    state_copy(head_sibling, other, slot_sibling, sibling).start()
    self_state.start()
    send_all(keys_copy)
    self_keys.start()
    send_all(values_copy)
    self_values.start()

    load_hyena.wait()
    product = (hy_v[1].astype(F32) * hy_v[2].astype(F32)).astype(BF16).astype(F32)
    padded[0:positions, :] = jnp.zeros((positions, channels), F32)
    padded[positions:, :] = product
    for load in small[1:]:
        load.wait()
    mixed[...] = skip_v[...] * product
    row_index = lax.broadcasted_iota(jnp.int32, (positions, vocab), 0)
    codes = jnp.zeros((positions, vocab), jnp.int32)
    for t in range(positions):
        codes = jnp.where(row_index == t, bases_s[t], codes)
    codes = jnp.where(row_index == pos_s[0], allele_s[0], codes)
    wanted = jnp.zeros((positions, vocab), jnp.int32)
    for code, token in enumerate(BASE_TOKENS):
        wanted = jnp.where(codes == code, token, wanted)
    targets[...] = wanted

    away = (3, n - 3)

    def gather_copy(side):
        return remote(
            q_own,
            gathered.at[side],
            gather_send.at[side],
            gather_recv.at[side],
            ring_device(away[side]),
        )

    wait_for(q_own.at[0 : heads - 1], spread_recv.at[0])
    self_q.wait()
    for side in range(2):
        gather_copy(side).start()

    wait_for(state_all.at[0, 0 : heads - 1], spread_recv.at[1])
    self_state.wait()
    state_mine = state_all.at[ring]

    def send_state_on(k, carry):
        remote(
            state_mine, state_mine, spread_send.at[3], spread_recv.at[3], ring_device(k)
        ).start()
        return carry

    lax.fori_loop(1, n, send_state_on, 0)

    load_filter.wait()

    def own_taps(h, carry):
        lanes = lanes_of(h)
        coeffs = jnp.transpose(filt_v[lanes, :])
        total = mixed[:, lanes]
        for j in range(1, positions):
            total = total + padded[positions - j : 2 * positions - j, lanes] * coeffs[j - 1 : j, :]
        mixed[:, lanes] = total
        return carry

    lax.fori_loop(0, heads, own_taps, 0)

    right = ring_device(1)
    left = ring_device(n - 1)

    def exchange(ref, send_sem, recv_sem):
        return (
            remote(ref.at[1], ref.at[0], send_sem.at[0], recv_sem.at[0], right),
            remote(ref.at[1], ref.at[2], send_sem.at[1], recv_sem.at[1], left),
        )

    wait_for(keys.at[1, 0 : heads - 1], spread_recv.at[2])
    self_keys.wait()
    keys_on = exchange(keys, keys_send, keys_recv)
    for copy in keys_on:
        copy.start()

    wait_for(values_own.at[0 : heads - 1], spread_recv.at[4])
    self_values.wait()
    block = values_own.shape[1]
    context = heads * block
    values_t[1] = jnp.transpose(values_own[...].reshape(context, HEAD_DIM))
    values_on = exchange(values_t, values_send, values_recv)
    for copy in values_on:
        copy.start()

    taps_own[...] = jnp.transpose(filt_v[lanes_of(head), :])
    state_rows[taps:, :] = jnp.zeros((positions, HEAD_DIM), F32)
    wait_for(state_all.at[0 : n - 1], spread_recv.at[3])

    for at in range(n):
        for slot in range(heads):
            spot, bit = divmod(slot, 2)
            row_z = (4 * at + 2 * (spot % 2) + bit) * (n // 2) + spot // 2
            row_y = (4 * spot + 2 * (at % 2) + bit) * (n // 2) + at // 2
            row = row_z + core * (row_y - row_z)
            state_rows[pl.ds(row, 1), :] = state_all[at, slot]

    def state_taps(step, total):
        base = pl.multiple_of(step * 8, 8)
        for b in range(8):
            total = total + (
                state_rows[pl.ds(base + b, positions), :]
                * taps_own[pl.ds(taps - 1 - b - base, 1), :]
            )
        return total

    state_part[...] = lax.fori_loop(
        0, taps // 8, state_taps, jnp.zeros((positions, HEAD_DIM), F32)
    ).astype(BF16)

    def back_device(k, core_to):
        spot = lax.rem(other + k, n)
        return (
            2 * spot + core_to,
            device((1 - core) * z + core * spot, (1 - core) * spot + core * y, core_to),
        )

    slot_beside = 2 * other + 1 - core

    def state_back(device_id):
        return remote(
            state_part, state_parts.at[head], back_send.at[0], back_recv.at[0], device_id
        )

    def send_state_back(k, carry):
        for core_to in range(2):
            state_back(back_device(k, core_to)[1]).start()
        return carry

    lax.fori_loop(1, n, send_state_back, 0)
    state_back(sibling).start()
    state_parts[head] = state_part[...]

    def merge(a, b):
        peak = jnp.maximum(a[1], b[1])
        scale_a = jnp.exp2((a[1] - peak) * EXP_SCALE)
        scale_b = jnp.exp2((b[1] - peak) * EXP_SCALE)
        return (a[0] * scale_a + b[0] * scale_b, peak, a[2] * scale_a + b[2] * scale_b)

    def attend(chunk, place, first=0, last=heads):
        from_keys = keys[place, first:last].reshape((last - first) * block, HEAD_DIM)
        from_values = values_t[place, :, first * block : last * block]
        numer, peak, total = [], [], []
        width = min(256, rows)
        for start in range(0, rows, width):
            part = chunk[start : start + width]
            scores = lax.dot_general(
                from_keys, part, (((1,), (1,)), ((), ())), preferred_element_type=F32
            )
            top = jnp.max(scores, 0, keepdims=True)
            weights = jnp.exp2((scores - top) * EXP_SCALE)
            peak.append(top)
            total.append(jnp.sum(weights, 0, keepdims=True))
            numer.append(jnp.dot(from_values, weights.astype(BF16), preferred_element_type=F32))
        return (
            jnp.concatenate(numer, 1),
            jnp.concatenate(peak, 1),
            jnp.concatenate(total, 1),
        )

    def chunk_of(index):
        ref = q_own if index == 2 else gathered.at[index]
        return ref[...].reshape(rows, HEAD_DIM)

    def store_sums(index, sums):
        sum_numer[index] = sums[0]
        sum_stat[index, 0:1, :] = sums[1]
        sum_stat[index, 1:2, :] = sums[2]

    def load_sums(index):
        return (sum_numer[index], sum_stat[index, 0:1, :], sum_stat[index, 1:2, :])

    store_sums(2, attend(chunk_of(2), 1))
    for side in range(2):
        gather_copy(side).wait_recv()
        store_sums(side, attend(chunk_of(side), 1))

    def part_copy(side):
        return remote(
            part_out.at[side],
            part_in.at[side],
            part_send.at[side],
            part_recv.at[side],
            ring_device(away[1 - side]),
        )

    def stat_copy(side):
        return remote(
            stat_out.at[side],
            stat_in.at[side],
            stat_send.at[side],
            stat_recv.at[side],
            ring_device(away[1 - side]),
        )

    for copy in keys_on + values_on:
        copy.wait_recv()
    middle = heads // 2
    for side in range(2):
        near_place, far_place = (0, 2) if side == 0 else (2, 0)
        far_first, far_last = (0, middle) if side == 0 else (middle, heads)
        sums = merge(load_sums(side), attend(chunk_of(side), near_place))
        sums = merge(sums, attend(chunk_of(side), far_place, far_first, far_last))
        part_out[side] = sums[0].astype(BF16)
        stat_out[side, 0:1, :] = sums[1]
        stat_out[side, 1:2, :] = sums[2]
        part_copy(side).start()
        stat_copy(side).start()
    sums = merge(load_sums(2), attend(chunk_of(2), 0))
    store_sums(2, merge(sums, attend(chunk_of(2), 2)))

    wait_for(state_parts.at[0 : heads - 1], back_recv.at[0])
    for h in range(heads):
        lanes = slice(h * HEAD_DIM, (h + 1) * HEAD_DIM)
        hyena_ref[0, :, lanes] = (
            hy_v[0, :, lanes].astype(F32) * (mixed[:, lanes] + state_parts[h].astype(F32))
        ).astype(BF16)
    load_keys.wait()
    group = HEAD_DIM // positions
    own = []
    row_at = lax.broadcasted_iota(jnp.int32, (HEAD_DIM, HEAD_DIM), 0)
    col_at = lax.broadcasted_iota(jnp.int32, (HEAD_DIM, HEAD_DIM), 1)
    seen = (lax.div(row_at, positions) == lax.div(col_at, positions)) & (col_at <= row_at)

    def stacked(ref, g):
        return jnp.concatenate(
            [ref[:, h * HEAD_DIM : (h + 1) * HEAD_DIM] for h in range(g * group, (g + 1) * group)],
            0,
        )

    for g in range(heads // group):
        scores = lax.dot_general(
            stacked(q_v, g), stacked(ck_v, g), (((1,), (1,)), ((), ())), preferred_element_type=F32
        )
        scores = jnp.where(seen, scores, LOWEST)
        top = jnp.max(scores, 1, keepdims=True)
        weights = jnp.where(seen, jnp.exp2((scores - top) * EXP_SCALE), 0.0)
        total = jnp.sum(weights, 1, keepdims=True)
        numer = jnp.dot(
            weights.astype(BF16), stacked(hyena_ref.at[0], g), preferred_element_type=F32
        )
        own.append((numer, top, total))

    mine = load_sums(2)
    for side in range(2):
        part_copy(side).wait_recv()
        stat_copy(side).wait_recv()
        mine = merge(
            mine,
            (part_in[side].astype(F32), stat_in[side, 0:1, :], stat_in[side, 1:2, :]),
        )
    numer, peak, total = mine
    merged[...] = jnp.transpose(numer).astype(BF16).reshape(merged.shape)
    for b in range(rows // HEAD_DIM):
        merged_stat[b, 0:1, :] = peak[:, b * HEAD_DIM : (b + 1) * HEAD_DIM]
        merged_stat[b, 1:2, :] = total[:, b * HEAD_DIM : (b + 1) * HEAD_DIM]

    def back_copy(slot, device_id):
        return remote(
            merged.at[slot], back.at[head], back_send.at[1], back_recv.at[1], device_id
        )

    def back_stat_copy(slot, device_id):
        return remote(
            merged_stat.at[lax.div(slot, group)],
            back_stat.at[head],
            back_send.at[2],
            back_recv.at[2],
            device_id,
        )

    def send_back(k, carry):
        for core_to in range(2):
            slot, device_id = back_device(k, core_to)
            back_copy(slot, device_id).start()
            back_stat_copy(slot, device_id).start()
        return carry

    lax.fori_loop(1, n, send_back, 0)
    back_copy(slot_beside, sibling).start()
    back_stat_copy(slot_beside, sibling).start()
    back[head] = merged[slot_self]
    back_stat[head] = merged_stat[lax.div(slot_self, group)]

    load_unembed.wait()
    stat_square[...] = jnp.zeros_like(stat_square)
    wait_for(back_stat.at[0 : heads - 1], back_recv.at[2])
    for first, slot in ((0, slot_y), (n, slot_z)):
        shift = lax.rem(HEAD_DIM - lax.rem(slot, group) * positions, HEAD_DIM)
        for kind in range(2):
            stat_square[kind * heads + first : kind * heads + first + n, :] = pltpu.roll(
                back_stat[first : first + n, kind, :], shift, 1
            )
    columns = jnp.transpose(stat_square[...])
    wait_for(back.at[0 : heads - 1], back_recv.at[1])
    pieces = []
    for g in range(heads // group):
        chosen = range(g * group, (g + 1) * group)
        peak = jnp.concatenate([columns[0:positions, h : h + 1] for h in chosen], 0)
        total = jnp.concatenate(
            [columns[0:positions, heads + h : heads + h + 1] for h in chosen], 0
        )
        numer = back[g * group : (g + 1) * group].reshape(HEAD_DIM, HEAD_DIM).astype(F32)
        numer, _, total = merge((numer, peak, total), own[g])
        attended = numer / total
        pieces += [attended[i * positions : (i + 1) * positions] for i in range(group)]
    attended = jnp.concatenate(pieces, 1)
    high = attended.astype(BF16)
    low = (attended - high.astype(F32)).astype(BF16)
    both = jnp.dot(
        jnp.concatenate([high, low], 0), unembed_v[...], preferred_element_type=F32
    )
    logit_parts[tp] = (both[0:positions] + both[positions:]).astype(BF16)

    tp_copies = [
        remote(
            logit_parts.at[tp],
            logit_parts.at[tp],
            tp_send,
            tp_recv,
            {"tp": lax.rem(tp + k, tp_count)},
        )
        for k in range(1, tp_count)
    ]
    for copy in tp_copies:
        copy.start()
    if tp_count > 1:
        wait_for(logit_parts.at[0 : tp_count - 1], tp_recv)
    logits = logit_parts[0].astype(F32)
    for k in range(1, tp_count):
        logits = logits + logit_parts[k].astype(F32)
    top = jnp.max(logits, 1, keepdims=True)
    log_total = top + jnp.log(jnp.sum(jnp.exp(logits - top), 1, keepdims=True))
    vocab_at = lax.broadcasted_iota(jnp.int32, (positions, vocab), 1)
    picked = jnp.sum(jnp.where(vocab_at == targets[...], logits, 0.0), 1, keepdims=True)
    log_probs = picked - log_total
    place = lax.broadcasted_iota(jnp.int32, (positions, positions), 0)
    lane = lax.broadcasted_iota(jnp.int32, (positions, positions), 1)
    log_row = jnp.sum(jnp.where(place == lane, log_probs, 0.0), 0, keepdims=True)
    log_probs_ref[...] = log_row
    lane_row = lax.broadcasted_iota(jnp.int32, (1, positions), 1)
    score_ref[...] = jnp.sum(
        jnp.where(lane_row < length_s[0], log_row, 0.0), 1, keepdims=True
    )

    wait_for(q_own.at[0 : heads - 1], spread_send.at[0])
    wait_for(state_all.at[0, 0 : heads - 1], spread_send.at[1])
    wait_for(keys.at[1, 0 : heads - 1], spread_send.at[2])
    wait_for(values_own.at[0 : heads - 1], spread_send.at[4])
    wait_for(state_all.at[0 : n - 1], spread_send.at[3])
    for copy in keys_on + values_on:
        copy.wait_send()
    for side in range(2):
        gather_copy(side).wait_send()
        part_copy(side).wait_send()
        stat_copy(side).wait_send()
    wait_for(state_parts.at[0 : heads - 1], back_send.at[0])
    wait_for(back.at[0 : heads - 1], back_send.at[1])
    wait_for(back_stat.at[0 : heads - 1], back_send.at[2])
    if tp_count > 1:
        wait_for(logit_parts.at[0 : tp_count - 1], tp_send)


def on_device(
    n,
    tp_count,
    context_kv,
    queries,
    cont_keys,
    hyena_inputs,
    hyena_state,
    hyena_filter,
    filter_skip,
    unembed,
    ref_bases,
    variant_pos,
    allele_ids,
    cont_lengths,
):
    positions, channels = queries.shape[1:]
    block = context_kv.shape[1]
    taps = hyena_filter.shape[1]
    vocab = unembed.shape[1]
    heads = channels // HEAD_DIM
    rows = heads * positions
    vmem = pltpu.VMEM
    dma = pltpu.SemaphoreType.DMA
    scratch = [
        vmem((heads, positions, HEAD_DIM), BF16),
        vmem((3, heads, block, HEAD_DIM), BF16),
        vmem((heads, block, HEAD_DIM), BF16),
        vmem((3, HEAD_DIM, heads * block), BF16),
        vmem((heads, 1, HEAD_DIM), F32),
        vmem((n, heads, 1, HEAD_DIM), F32),
        vmem((taps + positions, HEAD_DIM), F32),
        vmem((2, heads, positions, HEAD_DIM), BF16),
        vmem((2, HEAD_DIM, rows), BF16),
        vmem((2, 2, rows), F32),
        vmem((2, HEAD_DIM, rows), BF16),
        vmem((2, 2, rows), F32),
        vmem((3, HEAD_DIM, rows), F32),
        vmem((3, 2, rows), F32),
        vmem((heads, positions, HEAD_DIM), BF16),
        vmem((rows // HEAD_DIM, 2, HEAD_DIM), F32),
        vmem((heads, positions, HEAD_DIM), BF16),
        vmem((heads, 2, HEAD_DIM), F32),
        vmem((positions, HEAD_DIM), BF16),
        vmem((heads, positions, HEAD_DIM), BF16),
        vmem((HEAD_DIM, HEAD_DIM), F32),
        vmem((tp_count, positions, vocab), BF16),
        vmem((positions, vocab), jnp.int32),
        vmem((2 * positions, channels), F32),
        vmem((positions, channels), F32),
        vmem((taps, HEAD_DIM), F32),
        vmem((positions, channels), BF16),
        vmem((2, block, channels), BF16),
        vmem((positions, channels), BF16),
        vmem((3, positions, channels), BF16),
        vmem((channels, taps), F32),
        vmem((channels, vocab), BF16),
        vmem((1, channels), BF16),
        vmem((1, channels), F32),
        pltpu.SMEM((positions,), jnp.int32),
        pltpu.SMEM((1,), jnp.int32),
        pltpu.SMEM((1,), jnp.int32),
        pltpu.SMEM((1,), jnp.int32),
        dma((16,)),
        dma((5,)),
        dma((5,)),
        dma((2,)),
        dma((2,)),
        dma((2,)),
        dma((2,)),
        dma((2,)),
        dma((2,)),
        dma((2,)),
        dma((2,)),
        dma((2,)),
        dma((2,)),
        dma((3,)),
        dma((3,)),
        dma,
        dma,
    ]
    hbm = pl.BlockSpec(memory_space=pltpu.HBM)
    in_vmem = pl.BlockSpec(memory_space=pltpu.VMEM)
    hyena_out, log_probs, score = pl.pallas_call(
        functools.partial(spread_kernel, n, tp_count),
        out_shape=(
            jax.ShapeDtypeStruct((1, positions, channels), BF16),
            jax.ShapeDtypeStruct((1, positions), F32),
            jax.ShapeDtypeStruct((1, 1), F32),
        ),
        in_specs=[hbm] * 12,
        out_specs=(in_vmem, in_vmem, in_vmem),
        scratch_shapes=scratch,
        compiler_params=pltpu.CompilerParams(
            collective_id=0, has_side_effects=True, vmem_limit_bytes=60 * 1024 * 1024
        ),
    )(
        context_kv,
        queries,
        cont_keys,
        hyena_inputs,
        hyena_state,
        hyena_filter,
        filter_skip.reshape(1, channels),
        unembed,
        ref_bases,
        variant_pos,
        allele_ids,
        cont_lengths,
    )
    return hyena_out, log_probs, score.reshape(1)


def solution(mesh):
    n = mesh.shape["ctx"] // 4
    placed = (
        P(None, ("ctx", "var"), "tp"),
        P(("ctx", "var"), None, "tp"),
        P(("ctx", "var"), None, "tp"),
        P(None, ("ctx", "var"), None, "tp"),
        P(("ctx", "var"), "tp"),
        P("tp", None),
        P("tp"),
        P("tp", None),
        P(),
        P(("ctx", "var")),
        P(("ctx", "var")),
        P(("ctx", "var")),
    )
    return jax.shard_map(
        functools.partial(on_device, n, mesh.shape["tp"]),
        mesh=mesh,
        in_specs=placed,
        out_specs=(P(("ctx", "var"), None, "tp"), P(("ctx", "var"), None), P(("ctx", "var"))),
        check_vma=False,
    )
```

```python
import functools
import math

import jax
import jax.numpy as jnp
from jax import lax
from jax.experimental import pallas as pl
from jax.experimental.pallas import tpu as pltpu
from jax.sharding import PartitionSpec as P

HEAD_DIM = 128
BASE_TOKENS = (65, 67, 71, 84)
EXP_SCALE = HEAD_DIM ** (-0.5) * math.log2(math.e)
LOWEST = -3.0e38
BF16 = jnp.bfloat16
F32 = jnp.float32


def spread_kernel(
    n,
    tp_count,
    kv_ref,
    q_ref,
    ck_ref,
    hy_ref,
    state_ref,
    filt_ref,
    skip_ref,
    unembed_ref,
    bases_ref,
    pos_ref,
    allele_ref,
    length_ref,
    hyena_ref,
    log_probs_ref,
    score_ref,
    q_own,
    keys,
    values_own,
    values_t,
    state_src,
    state_all,
    state_rows,
    gathered,
    part_out,
    stat_out,
    part_in,
    stat_in,
    sum_numer,
    sum_stat,
    weights_kept,
    merged,
    merged_stat,
    back,
    back_stat,
    state_part,
    state_parts,
    stat_square,
    logit_parts,
    targets,
    padded,
    mixed,
    taps_own,
    q_v,
    kv_v,
    ck_v,
    hy_v,
    filt_v,
    unembed_v,
    state_v,
    skip_v,
    bases_s,
    pos_s,
    allele_s,
    length_s,
    local_sem,
    spread_send,
    spread_recv,
    gather_send,
    gather_recv,
    part_send,
    part_recv,
    stat_send,
    stat_recv,
    keys_send,
    keys_recv,
    values_send,
    values_recv,
    back_send,
    back_recv,
    tp_send,
    tp_recv,
):
    heads = 2 * n
    positions = q_v.shape[0]
    rows = heads * positions
    taps = filt_v.shape[1]
    channels = heads * HEAD_DIM
    vocab = unembed_v.shape[1]

    ctx = lax.axis_index("ctx")
    var = lax.axis_index("var")
    tp = lax.axis_index("tp")
    z = lax.div(ctx, 4)
    core = lax.rem(ctx, 2)
    y = var * 2 + lax.div(lax.rem(ctx, 4), 2)
    ring = (1 - core) * z + core * y
    other = (1 - core) * y + core * z
    head = (1 - core) * y + core * (n + z)

    def device(z_to, y_to, core_to):
        return {"ctx": z_to * 4 + lax.rem(y_to, 2) * 2 + core_to, "var": lax.div(y_to, 2)}

    def ring_device(offset):
        return device(
            lax.rem(z + offset * (1 - core), n), lax.rem(y + offset * core, n), core
        )

    sibling = device(z, y, 1 - core)

    def remote(src, dst, send_sem, recv_sem, device_id):
        return pltpu.make_async_remote_copy(
            src_ref=src,
            dst_ref=dst,
            send_sem=send_sem,
            recv_sem=recv_sem,
            device_id=device_id,
            device_id_type=pl.DeviceIdType.MESH,
        )

    def wait_for(ref, sem):
        pltpu.make_async_copy(ref, ref, sem).wait()

    def lanes_of(h):
        return pl.ds(pl.multiple_of(h * HEAD_DIM, HEAD_DIM), HEAD_DIM)

    barrier = pltpu.get_barrier_semaphore()

    def greet(device_id):
        pl.semaphore_signal(
            barrier, inc=1, device_id=device_id, device_id_type=pl.DeviceIdType.MESH
        )

    def greet_offset(k, carry):
        for core_to in range(2):
            greet(device(z, lax.rem(y + k, n), core_to))
            greet(device(lax.rem(z + k, n), y, core_to))
        return carry

    lax.fori_loop(1, n, greet_offset, 0)
    greet(sibling)
    for k in range(1, tp_count):
        greet({"tp": lax.rem(tp + k, tp_count)})

    small = [
        pltpu.make_async_copy(src, dst, local_sem.at[8 + i])
        for i, (src, dst) in enumerate(
            (
                (state_ref, state_v),
                (skip_ref, skip_v),
                (bases_ref, bases_s),
                (pos_ref, pos_s),
                (allele_ref, allele_s),
                (length_ref, length_s),
            )
        )
    ]
    for load in small:
        load.start()
    load_q = pltpu.make_async_copy(q_ref.at[0], q_v, local_sem.at[2])
    load_kv = pltpu.make_async_copy(kv_ref, kv_v, local_sem.at[14])
    load_hyena = pltpu.make_async_copy(hy_ref.at[:, 0], hy_v, local_sem.at[0])
    load_filter = pltpu.make_async_copy(filt_ref, filt_v, local_sem.at[1])
    load_keys = pltpu.make_async_copy(ck_ref.at[0], ck_v, local_sem.at[3])
    load_unembed = pltpu.make_async_copy(unembed_ref, unembed_v, local_sem.at[4])
    for load in (load_q, load_kv, load_hyena, load_filter, load_keys, load_unembed):
        load.start()

    small[0].wait()
    for h in range(heads):
        state_src[h] = state_v[:, h * HEAD_DIM : (h + 1) * HEAD_DIM].astype(F32)
    load_q.wait()
    load_kv.wait()
    pl.semaphore_wait(barrier, 4 * (n - 1) + 1 + tp_count - 1)

    slot_y = 2 * y + core
    slot_z = 2 * z + core
    slot_self = 2 * other + core
    slot_sibling = 2 * ring + core
    head_sibling = (1 - core) * (n + z) + core * y

    def q_copy(h, slot, device_id):
        return remote(
            q_v.at[:, lanes_of(h)],
            q_own.at[slot],
            spread_send.at[0],
            spread_recv.at[0],
            device_id,
        )

    def state_copy(h, ring_to, slot, device_id):
        return remote(
            state_src.at[h],
            state_all.at[ring_to, slot],
            spread_send.at[1],
            spread_recv.at[1],
            device_id,
        )

    def keys_copy(h, slot, device_id):
        return remote(
            kv_v.at[0, :, lanes_of(h)],
            keys.at[1, slot],
            spread_send.at[2],
            spread_recv.at[2],
            device_id,
        )

    def values_copy(h, slot, device_id):
        return remote(
            kv_v.at[1, :, lanes_of(h)],
            values_own.at[slot],
            spread_send.at[4],
            spread_recv.at[4],
            device_id,
        )

    def send_all(copy):
        def send(k, carry):
            y_to = lax.rem(y + k, n)
            z_to = lax.rem(z + k, n)
            copy(y_to, slot_y, device(z, y_to, 0)).start()
            copy(n + z_to, slot_z, device(z_to, y, 1)).start()
            return carry

        lax.fori_loop(1, n, send, 0)
        copy(head_sibling, slot_sibling, sibling).start()

    def send_state(k, carry):
        y_to = lax.rem(y + k, n)
        z_to = lax.rem(z + k, n)
        state_copy(y_to, z, slot_y, device(z, y_to, 0)).start()
        state_copy(n + z_to, y, slot_z, device(z_to, y, 1)).start()
        return carry

    self_q = pltpu.make_async_copy(
        q_v.at[:, lanes_of(head)], q_own.at[slot_self], local_sem.at[5]
    )
    self_keys = pltpu.make_async_copy(
        kv_v.at[0, :, lanes_of(head)], keys.at[1, slot_self], local_sem.at[6]
    )
    self_values = pltpu.make_async_copy(
        kv_v.at[1, :, lanes_of(head)], values_own.at[slot_self], local_sem.at[15]
    )
    self_state = pltpu.make_async_copy(
        state_src.at[head], state_all.at[ring, slot_self], local_sem.at[7]
    )
    send_all(q_copy)
    self_q.start()
    lax.fori_loop(1, n, send_state, 0)
    state_copy(head_sibling, other, slot_sibling, sibling).start()
    self_state.start()
    send_all(keys_copy)
    self_keys.start()
    send_all(values_copy)
    self_values.start()

    load_hyena.wait()
    product = (hy_v[1].astype(F32) * hy_v[2].astype(F32)).astype(BF16).astype(F32)
    padded[0:positions, :] = jnp.zeros((positions, channels), F32)
    padded[positions:, :] = product
    for load in small[1:]:
        load.wait()
    mixed[...] = skip_v[...] * product
    row_index = lax.broadcasted_iota(jnp.int32, (positions, vocab), 0)
    codes = jnp.zeros((positions, vocab), jnp.int32)
    for t in range(positions):
        codes = jnp.where(row_index == t, bases_s[t], codes)
    codes = jnp.where(row_index == pos_s[0], allele_s[0], codes)
    wanted = jnp.zeros((positions, vocab), jnp.int32)
    for code, token in enumerate(BASE_TOKENS):
        wanted = jnp.where(codes == code, token, wanted)
    targets[...] = wanted

    away = (3, n - 3)

    def gather_copy(side):
        return remote(
            q_own,
            gathered.at[side],
            gather_send.at[side],
            gather_recv.at[side],
            ring_device(away[side]),
        )

    wait_for(q_own.at[0 : heads - 1], spread_recv.at[0])
    self_q.wait()
    for side in range(2):
        gather_copy(side).start()

    wait_for(state_all.at[0, 0 : heads - 1], spread_recv.at[1])
    self_state.wait()
    state_mine = state_all.at[ring]

    def send_state_on(k, carry):
        remote(
            state_mine, state_mine, spread_send.at[3], spread_recv.at[3], ring_device(k)
        ).start()
        return carry

    lax.fori_loop(1, n, send_state_on, 0)

    load_filter.wait()

    def own_taps(h, carry):
        lanes = lanes_of(h)
        coeffs = jnp.transpose(filt_v[lanes, :])
        total = mixed[:, lanes]
        for j in range(1, positions):
            total = total + padded[positions - j : 2 * positions - j, lanes] * coeffs[j - 1 : j, :]
        mixed[:, lanes] = total
        return carry

    lax.fori_loop(0, heads, own_taps, 0)

    right = ring_device(1)
    left = ring_device(n - 1)

    def exchange(ref, send_sem, recv_sem):
        return (
            remote(ref.at[1], ref.at[0], send_sem.at[0], recv_sem.at[0], right),
            remote(ref.at[1], ref.at[2], send_sem.at[1], recv_sem.at[1], left),
        )

    wait_for(keys.at[1, 0 : heads - 1], spread_recv.at[2])
    self_keys.wait()
    keys_on = exchange(keys, keys_send, keys_recv)
    for copy in keys_on:
        copy.start()

    wait_for(values_own.at[0 : heads - 1], spread_recv.at[4])
    self_values.wait()
    block = values_own.shape[1]
    context = heads * block
    values_t[1] = jnp.transpose(values_own[...].reshape(context, HEAD_DIM))
    values_on = exchange(values_t, values_send, values_recv)
    for copy in values_on:
        copy.start()

    taps_own[...] = jnp.transpose(filt_v[lanes_of(head), :])
    state_rows[taps:, :] = jnp.zeros((positions, HEAD_DIM), F32)
    wait_for(state_all.at[0 : n - 1], spread_recv.at[3])

    for at in range(n):
        for slot in range(heads):
            spot, bit = divmod(slot, 2)
            row_z = (4 * at + 2 * (spot % 2) + bit) * (n // 2) + spot // 2
            row_y = (4 * spot + 2 * (at % 2) + bit) * (n // 2) + at // 2
            row = row_z + core * (row_y - row_z)
            state_rows[pl.ds(row, 1), :] = state_all[at, slot]

    def state_taps(step, total):
        base = pl.multiple_of(step * 8, 8)
        for b in range(8):
            total = total + (
                state_rows[pl.ds(base + b, positions), :]
                * taps_own[pl.ds(taps - 1 - b - base, 1), :]
            )
        return total

    state_part[...] = lax.fori_loop(
        0, taps // 8, state_taps, jnp.zeros((positions, HEAD_DIM), F32)
    ).astype(BF16)

    def back_device(k, core_to):
        spot = lax.rem(other + k, n)
        return (
            2 * spot + core_to,
            device((1 - core) * z + core * spot, (1 - core) * spot + core * y, core_to),
        )

    slot_beside = 2 * other + 1 - core

    def state_back(device_id):
        return remote(
            state_part, state_parts.at[head], back_send.at[0], back_recv.at[0], device_id
        )

    def send_state_back(k, carry):
        for core_to in range(2):
            state_back(back_device(k, core_to)[1]).start()
        return carry

    lax.fori_loop(1, n, send_state_back, 0)
    state_back(sibling).start()
    state_parts[head] = state_part[...]

    def merge(a, b):
        peak = jnp.maximum(a[1], b[1])
        scale_a = jnp.exp2((a[1] - peak) * EXP_SCALE)
        scale_b = jnp.exp2((b[1] - peak) * EXP_SCALE)
        return (a[0] * scale_a + b[0] * scale_b, peak, a[2] * scale_a + b[2] * scale_b)

    def weigh(chunk, place, first=0, last=heads):
        from_keys = keys[place, first:last].reshape((last - first) * block, HEAD_DIM)
        weights, peak, total = [], [], []
        width = min(256, rows)
        for start in range(0, rows, width):
            part = chunk[start : start + width]
            scores = lax.dot_general(
                from_keys, part, (((1,), (1,)), ((), ())), preferred_element_type=F32
            )
            top = jnp.max(scores, 0, keepdims=True)
            weight = jnp.exp2((scores - top) * EXP_SCALE)
            weights.append(weight.astype(BF16))
            peak.append(top)
            total.append(jnp.sum(weight, 0, keepdims=True))
        return [jnp.concatenate(pieces, 1) for pieces in (weights, peak, total)]

    def apply(weights, place, first=0, last=heads):
        from_values = values_t[place, :, first * block : last * block]
        return jnp.dot(from_values, weights, preferred_element_type=F32)

    def attend(chunk, place):
        weights, peak, total = weigh(chunk, place)
        return apply(weights, place), peak, total

    def chunk_of(index):
        ref = q_own if index == 2 else gathered.at[index]
        return ref[...].reshape(rows, HEAD_DIM)

    def store_sums(index, sums):
        sum_numer[index] = sums[0]
        sum_stat[index, 0:1, :] = sums[1]
        sum_stat[index, 1:2, :] = sums[2]

    def load_sums(index):
        return (sum_numer[index], sum_stat[index, 0:1, :], sum_stat[index, 1:2, :])

    for side in range(2):
        gather_copy(side).wait_recv()
        store_sums(side, attend(chunk_of(side), 1))

    def part_copy(side):
        return remote(
            part_out.at[side],
            part_in.at[side],
            part_send.at[side],
            part_recv.at[side],
            ring_device(away[1 - side]),
        )

    def stat_copy(side):
        return remote(
            stat_out.at[side],
            stat_in.at[side],
            stat_send.at[side],
            stat_recv.at[side],
            ring_device(away[1 - side]),
        )

    middle = heads // 2
    spans = (
        ((0, 0, heads), (2, 0, middle)),
        ((2, 0, heads), (0, middle, heads)),
        ((0, 0, heads), (2, 0, heads)),
    )
    for copy in keys_on:
        copy.wait_recv()
    stats = []
    for index in range(2):
        for which, (place, first, last) in enumerate(spans[index]):
            weights, peak, total = weigh(chunk_of(index), place, first, last)
            weights_kept[index, which, 0 : (last - first) * block, :] = weights
            stats.append((peak, total))

    def finish(index):
        sums = load_sums(index)
        for which, (place, first, last) in enumerate(spans[index]):
            numer = apply(
                weights_kept[index, which, 0 : (last - first) * block, :], place, first, last
            )
            sums = merge(sums, (numer, *stats[2 * index + which]))
        return sums

    for copy in values_on:
        copy.wait_recv()
    for side in range(2):
        sums = finish(side)
        part_out[side] = sums[0].astype(BF16)
        stat_out[side, 0:1, :] = sums[1]
        stat_out[side, 1:2, :] = sums[2]
        part_copy(side).start()
        stat_copy(side).start()
    store_sums(2, attend(chunk_of(2), 1))
    for place, first, last in spans[2]:
        store_sums(2, merge(load_sums(2), attend(chunk_of(2), place)))

    wait_for(state_parts.at[0 : heads - 1], back_recv.at[0])
    for h in range(heads):
        lanes = slice(h * HEAD_DIM, (h + 1) * HEAD_DIM)
        hyena_ref[0, :, lanes] = (
            hy_v[0, :, lanes].astype(F32) * (mixed[:, lanes] + state_parts[h].astype(F32))
        ).astype(BF16)
    load_keys.wait()
    group = HEAD_DIM // positions
    own = []
    row_at = lax.broadcasted_iota(jnp.int32, (HEAD_DIM, HEAD_DIM), 0)
    col_at = lax.broadcasted_iota(jnp.int32, (HEAD_DIM, HEAD_DIM), 1)
    seen = (lax.div(row_at, positions) == lax.div(col_at, positions)) & (col_at <= row_at)

    def stacked(ref, g):
        return jnp.concatenate(
            [ref[:, h * HEAD_DIM : (h + 1) * HEAD_DIM] for h in range(g * group, (g + 1) * group)],
            0,
        )

    for g in range(heads // group):
        scores = lax.dot_general(
            stacked(q_v, g), stacked(ck_v, g), (((1,), (1,)), ((), ())), preferred_element_type=F32
        )
        scores = jnp.where(seen, scores, LOWEST)
        top = jnp.max(scores, 1, keepdims=True)
        weights = jnp.where(seen, jnp.exp2((scores - top) * EXP_SCALE), 0.0)
        total = jnp.sum(weights, 1, keepdims=True)
        numer = jnp.dot(
            weights.astype(BF16), stacked(hyena_ref.at[0], g), preferred_element_type=F32
        )
        own.append((numer, top, total))

    mine = load_sums(2)
    for side in range(2):
        part_copy(side).wait_recv()
        stat_copy(side).wait_recv()
        mine = merge(
            mine,
            (part_in[side].astype(F32), stat_in[side, 0:1, :], stat_in[side, 1:2, :]),
        )
    numer, peak, total = mine
    merged[...] = jnp.transpose(numer).astype(BF16).reshape(merged.shape)
    for b in range(rows // HEAD_DIM):
        merged_stat[b, 0:1, :] = peak[:, b * HEAD_DIM : (b + 1) * HEAD_DIM]
        merged_stat[b, 1:2, :] = total[:, b * HEAD_DIM : (b + 1) * HEAD_DIM]

    def back_copy(slot, device_id):
        return remote(
            merged.at[slot], back.at[head], back_send.at[1], back_recv.at[1], device_id
        )

    def back_stat_copy(slot, device_id):
        return remote(
            merged_stat.at[lax.div(slot, group)],
            back_stat.at[head],
            back_send.at[2],
            back_recv.at[2],
            device_id,
        )

    def send_back(k, carry):
        for core_to in range(2):
            slot, device_id = back_device(k, core_to)
            back_copy(slot, device_id).start()
            back_stat_copy(slot, device_id).start()
        return carry

    lax.fori_loop(1, n, send_back, 0)
    back_copy(slot_beside, sibling).start()
    back_stat_copy(slot_beside, sibling).start()
    back[head] = merged[slot_self]
    back_stat[head] = merged_stat[lax.div(slot_self, group)]

    load_unembed.wait()
    stat_square[...] = jnp.zeros_like(stat_square)
    wait_for(back_stat.at[0 : heads - 1], back_recv.at[2])
    for first, slot in ((0, slot_y), (n, slot_z)):
        shift = lax.rem(HEAD_DIM - lax.rem(slot, group) * positions, HEAD_DIM)
        for kind in range(2):
            stat_square[kind * heads + first : kind * heads + first + n, :] = pltpu.roll(
                back_stat[first : first + n, kind, :], shift, 1
            )
    columns = jnp.transpose(stat_square[...])
    wait_for(back.at[0 : heads - 1], back_recv.at[1])
    pieces = []
    for g in range(heads // group):
        chosen = range(g * group, (g + 1) * group)
        peak = jnp.concatenate([columns[0:positions, h : h + 1] for h in chosen], 0)
        total = jnp.concatenate(
            [columns[0:positions, heads + h : heads + h + 1] for h in chosen], 0
        )
        numer = back[g * group : (g + 1) * group].reshape(HEAD_DIM, HEAD_DIM).astype(F32)
        numer, _, total = merge((numer, peak, total), own[g])
        attended = numer / total
        pieces += [attended[i * positions : (i + 1) * positions] for i in range(group)]
    attended = jnp.concatenate(pieces, 1)
    high = attended.astype(BF16)
    low = (attended - high.astype(F32)).astype(BF16)
    both = jnp.dot(
        jnp.concatenate([high, low], 0), unembed_v[...], preferred_element_type=F32
    )
    logit_parts[tp] = (both[0:positions] + both[positions:]).astype(BF16)

    tp_copies = [
        remote(
            logit_parts.at[tp],
            logit_parts.at[tp],
            tp_send,
            tp_recv,
            {"tp": lax.rem(tp + k, tp_count)},
        )
        for k in range(1, tp_count)
    ]
    for copy in tp_copies:
        copy.start()
    if tp_count > 1:
        wait_for(logit_parts.at[0 : tp_count - 1], tp_recv)
    logits = logit_parts[0].astype(F32)
    for k in range(1, tp_count):
        logits = logits + logit_parts[k].astype(F32)
    top = jnp.max(logits, 1, keepdims=True)
    log_total = top + jnp.log(jnp.sum(jnp.exp(logits - top), 1, keepdims=True))
    vocab_at = lax.broadcasted_iota(jnp.int32, (positions, vocab), 1)
    picked = jnp.sum(jnp.where(vocab_at == targets[...], logits, 0.0), 1, keepdims=True)
    log_probs = picked - log_total
    place = lax.broadcasted_iota(jnp.int32, (positions, positions), 0)
    lane = lax.broadcasted_iota(jnp.int32, (positions, positions), 1)
    log_row = jnp.sum(jnp.where(place == lane, log_probs, 0.0), 0, keepdims=True)
    log_probs_ref[...] = log_row
    lane_row = lax.broadcasted_iota(jnp.int32, (1, positions), 1)
    score_ref[...] = jnp.sum(
        jnp.where(lane_row < length_s[0], log_row, 0.0), 1, keepdims=True
    )

    wait_for(q_own.at[0 : heads - 1], spread_send.at[0])
    wait_for(state_all.at[0, 0 : heads - 1], spread_send.at[1])
    wait_for(keys.at[1, 0 : heads - 1], spread_send.at[2])
    wait_for(values_own.at[0 : heads - 1], spread_send.at[4])
    wait_for(state_all.at[0 : n - 1], spread_send.at[3])
    for copy in keys_on + values_on:
        copy.wait_send()
    for side in range(2):
        gather_copy(side).wait_send()
        part_copy(side).wait_send()
        stat_copy(side).wait_send()
    wait_for(state_parts.at[0 : heads - 1], back_send.at[0])
    wait_for(back.at[0 : heads - 1], back_send.at[1])
    wait_for(back_stat.at[0 : heads - 1], back_send.at[2])
    if tp_count > 1:
        wait_for(logit_parts.at[0 : tp_count - 1], tp_send)


def on_device(
    n,
    tp_count,
    context_kv,
    queries,
    cont_keys,
    hyena_inputs,
    hyena_state,
    hyena_filter,
    filter_skip,
    unembed,
    ref_bases,
    variant_pos,
    allele_ids,
    cont_lengths,
):
    positions, channels = queries.shape[1:]
    block = context_kv.shape[1]
    taps = hyena_filter.shape[1]
    vocab = unembed.shape[1]
    heads = channels // HEAD_DIM
    rows = heads * positions
    vmem = pltpu.VMEM
    dma = pltpu.SemaphoreType.DMA
    scratch = [
        vmem((heads, positions, HEAD_DIM), BF16),
        vmem((3, heads, block, HEAD_DIM), BF16),
        vmem((heads, block, HEAD_DIM), BF16),
        vmem((3, HEAD_DIM, heads * block), BF16),
        vmem((heads, 1, HEAD_DIM), F32),
        vmem((n, heads, 1, HEAD_DIM), F32),
        vmem((taps + positions, HEAD_DIM), F32),
        vmem((2, heads, positions, HEAD_DIM), BF16),
        vmem((2, HEAD_DIM, rows), BF16),
        vmem((2, 2, rows), F32),
        vmem((2, HEAD_DIM, rows), BF16),
        vmem((2, 2, rows), F32),
        vmem((3, HEAD_DIM, rows), F32),
        vmem((3, 2, rows), F32),
        vmem((3, 2, heads * block, rows), BF16),
        vmem((heads, positions, HEAD_DIM), BF16),
        vmem((rows // HEAD_DIM, 2, HEAD_DIM), F32),
        vmem((heads, positions, HEAD_DIM), BF16),
        vmem((heads, 2, HEAD_DIM), F32),
        vmem((positions, HEAD_DIM), BF16),
        vmem((heads, positions, HEAD_DIM), BF16),
        vmem((HEAD_DIM, HEAD_DIM), F32),
        vmem((tp_count, positions, vocab), BF16),
        vmem((positions, vocab), jnp.int32),
        vmem((2 * positions, channels), F32),
        vmem((positions, channels), F32),
        vmem((taps, HEAD_DIM), F32),
        vmem((positions, channels), BF16),
        vmem((2, block, channels), BF16),
        vmem((positions, channels), BF16),
        vmem((3, positions, channels), BF16),
        vmem((channels, taps), F32),
        vmem((channels, vocab), BF16),
        vmem((1, channels), BF16),
        vmem((1, channels), F32),
        pltpu.SMEM((positions,), jnp.int32),
        pltpu.SMEM((1,), jnp.int32),
        pltpu.SMEM((1,), jnp.int32),
        pltpu.SMEM((1,), jnp.int32),
        dma((16,)),
        dma((5,)),
        dma((5,)),
        dma((2,)),
        dma((2,)),
        dma((2,)),
        dma((2,)),
        dma((2,)),
        dma((2,)),
        dma((2,)),
        dma((2,)),
        dma((2,)),
        dma((2,)),
        dma((3,)),
        dma((3,)),
        dma,
        dma,
    ]
    hbm = pl.BlockSpec(memory_space=pltpu.HBM)
    in_vmem = pl.BlockSpec(memory_space=pltpu.VMEM)
    stay = [
        pltpu.with_memory_space_constraint(array, pltpu.HBM)
        for array in (
            context_kv,
            queries,
            cont_keys,
            hyena_inputs,
            hyena_state,
            hyena_filter,
            filter_skip.reshape(1, channels),
            unembed,
            ref_bases,
        )
    ]
    hyena_out, log_probs, score = pl.pallas_call(
        functools.partial(spread_kernel, n, tp_count),
        out_shape=(
            jax.ShapeDtypeStruct((1, positions, channels), BF16),
            jax.ShapeDtypeStruct((1, positions), F32),
            jax.ShapeDtypeStruct((1, 1), F32),
        ),
        in_specs=[hbm] * 12,
        out_specs=(in_vmem, in_vmem, in_vmem),
        scratch_shapes=scratch,
        compiler_params=pltpu.CompilerParams(
            collective_id=0, has_side_effects=True, vmem_limit_bytes=48 * 1024 * 1024
        ),
    )(
        *stay,
        variant_pos,
        allele_ids,
        cont_lengths,
    )
    return hyena_out, log_probs, score.reshape(1)


def solution(mesh):
    n = mesh.shape["ctx"] // 4
    placed = (
        P(None, ("ctx", "var"), "tp"),
        P(("ctx", "var"), None, "tp"),
        P(("ctx", "var"), None, "tp"),
        P(None, ("ctx", "var"), None, "tp"),
        P(("ctx", "var"), "tp"),
        P("tp", None),
        P("tp"),
        P("tp", None),
        P(),
        P(("ctx", "var")),
        P(("ctx", "var")),
        P(("ctx", "var")),
    )
    return jax.shard_map(
        functools.partial(on_device, n, mesh.shape["tp"]),
        mesh=mesh,
        in_specs=placed,
        out_specs=(P(("ctx", "var"), None, "tp"), P(("ctx", "var"), None), P(("ctx", "var"))),
        check_vma=False,
    )
```

```python
import functools
import math

import jax
import jax.numpy as jnp
from jax import lax
from jax.experimental import pallas as pl
from jax.experimental.pallas import tpu as pltpu
from jax.sharding import PartitionSpec as P

HEAD_DIM = 128
BASE_TOKENS = (65, 67, 71, 84)
EXP_SCALE = HEAD_DIM ** (-0.5) * math.log2(math.e)
LOWEST = -3.0e38
BF16 = jnp.bfloat16
F32 = jnp.float32


def spread_kernel(
    n,
    tp_count,
    kv_ref,
    q_ref,
    ck_ref,
    hy_ref,
    state_ref,
    filt_ref,
    skip_ref,
    unembed_ref,
    bases_ref,
    pos_ref,
    allele_ref,
    length_ref,
    hyena_ref,
    log_probs_ref,
    score_ref,
    q_own,
    keys,
    values_own,
    values_t,
    state_src,
    state_all,
    state_rows,
    gathered,
    part_out,
    stat_out,
    part_in,
    stat_in,
    sum_numer,
    sum_stat,
    weights_kept,
    merged,
    merged_stat,
    back,
    back_stat,
    state_part,
    state_parts,
    stat_square,
    logit_parts,
    targets,
    padded,
    mixed,
    taps_own,
    q_v,
    kv_v,
    ck_v,
    hy_v,
    filt_v,
    unembed_v,
    state_v,
    skip_v,
    bases_s,
    pos_s,
    allele_s,
    length_s,
    local_sem,
    spread_send,
    spread_recv,
    gather_send,
    gather_recv,
    part_send,
    part_recv,
    stat_send,
    stat_recv,
    keys_send,
    keys_recv,
    values_send,
    values_recv,
    back_send,
    back_recv,
    tp_send,
    tp_recv,
):
    heads = 2 * n
    positions = q_v.shape[0]
    rows = heads * positions
    taps = filt_v.shape[1]
    group = HEAD_DIM // positions
    channels = heads * HEAD_DIM
    vocab = unembed_v.shape[1]

    ctx = lax.axis_index("ctx")
    var = lax.axis_index("var")
    tp = lax.axis_index("tp")
    z = lax.div(ctx, 4)
    core = lax.rem(ctx, 2)
    y = var * 2 + lax.div(lax.rem(ctx, 4), 2)
    ring = (1 - core) * z + core * y
    other = (1 - core) * y + core * z
    head = (1 - core) * y + core * (n + z)

    def device(z_to, y_to, core_to):
        return {"ctx": z_to * 4 + lax.rem(y_to, 2) * 2 + core_to, "var": lax.div(y_to, 2)}

    def ring_device(offset):
        return device(
            lax.rem(z + offset * (1 - core), n), lax.rem(y + offset * core, n), core
        )

    sibling = device(z, y, 1 - core)

    def remote(src, dst, send_sem, recv_sem, device_id):
        return pltpu.make_async_remote_copy(
            src_ref=src,
            dst_ref=dst,
            send_sem=send_sem,
            recv_sem=recv_sem,
            device_id=device_id,
            device_id_type=pl.DeviceIdType.MESH,
        )

    def wait_for(ref, sem):
        pltpu.make_async_copy(ref, ref, sem).wait()

    def farthest_first(send):
        def at(index, carry):
            step = lax.div(index + 1, 2) * (2 * lax.rem(index, 2) - 1)
            return send(n // 2 + step, carry)

        lax.fori_loop(0, n - 1, at, 0)

    def lanes_of(h):
        return pl.ds(pl.multiple_of(h * HEAD_DIM, HEAD_DIM), HEAD_DIM)

    barrier = pltpu.get_barrier_semaphore()

    def greet(device_id):
        pl.semaphore_signal(
            barrier, inc=1, device_id=device_id, device_id_type=pl.DeviceIdType.MESH
        )

    def greet_offset(k, carry):
        for core_to in range(2):
            greet(device(z, lax.rem(y + k, n), core_to))
            greet(device(lax.rem(z + k, n), y, core_to))
        return carry

    farthest_first(greet_offset)
    greet(sibling)
    for k in range(1, tp_count):
        greet({"tp": lax.rem(tp + k, tp_count)})

    small = [
        pltpu.make_async_copy(src, dst, local_sem.at[8 + i])
        for i, (src, dst) in enumerate(
            (
                (state_ref, state_v),
                (skip_ref, skip_v),
                (bases_ref, bases_s),
                (pos_ref, pos_s),
                (allele_ref, allele_s),
                (length_ref, length_s),
            )
        )
    ]
    for load in small:
        load.start()
    load_q = pltpu.make_async_copy(q_ref.at[0], q_v, local_sem.at[2])
    load_kv = pltpu.make_async_copy(kv_ref, kv_v, local_sem.at[14])
    load_hyena = pltpu.make_async_copy(hy_ref.at[:, 0], hy_v, local_sem.at[0])
    load_filter = pltpu.make_async_copy(filt_ref, filt_v, local_sem.at[1])
    load_keys = pltpu.make_async_copy(ck_ref.at[0], ck_v, local_sem.at[3])
    load_unembed = pltpu.make_async_copy(unembed_ref, unembed_v, local_sem.at[4])
    for load in (load_q, load_kv, load_hyena, load_filter, load_keys, load_unembed):
        load.start()

    small[0].wait()
    for h in range(heads):
        state_src[h] = state_v[:, h * HEAD_DIM : (h + 1) * HEAD_DIM].astype(F32)
    load_q.wait()
    load_kv.wait()
    pl.semaphore_wait(barrier, 4 * (n - 1) + 1 + tp_count - 1)

    slot_y = 2 * y + core
    slot_z = 2 * z + core
    slot_self = 2 * other + core
    slot_sibling = 2 * ring + core
    head_sibling = (1 - core) * (n + z) + core * y

    def q_copy(h, slot, device_id):
        return remote(
            q_v.at[:, lanes_of(h)],
            q_own.at[slot],
            spread_send.at[0],
            spread_recv.at[0],
            device_id,
        )

    def state_copy(h, ring_to, slot, device_id):
        return remote(
            state_src.at[h],
            state_all.at[ring_to, slot],
            spread_send.at[1],
            spread_recv.at[1],
            device_id,
        )

    def keys_copy(h, slot, device_id):
        return remote(
            kv_v.at[0, :, lanes_of(h)],
            keys.at[1, slot],
            spread_send.at[2],
            spread_recv.at[2],
            device_id,
        )

    def values_copy(h, slot, device_id):
        return remote(
            kv_v.at[1, :, lanes_of(h)],
            values_own.at[slot],
            spread_send.at[4],
            spread_recv.at[4],
            device_id,
        )

    def send_all(copy):
        def send(k, carry):
            y_to = lax.rem(y + k, n)
            z_to = lax.rem(z + k, n)
            copy(y_to, slot_y, device(z, y_to, 0)).start()
            copy(n + z_to, slot_z, device(z_to, y, 1)).start()
            return carry

        farthest_first(send)
        copy(head_sibling, slot_sibling, sibling).start()

    def send_state(k, carry):
        y_to = lax.rem(y + k, n)
        z_to = lax.rem(z + k, n)
        state_copy(y_to, z, slot_y, device(z, y_to, 0)).start()
        state_copy(n + z_to, y, slot_z, device(z_to, y, 1)).start()
        return carry

    self_q = pltpu.make_async_copy(
        q_v.at[:, lanes_of(head)], q_own.at[slot_self], local_sem.at[5]
    )
    self_keys = pltpu.make_async_copy(
        kv_v.at[0, :, lanes_of(head)], keys.at[1, slot_self], local_sem.at[6]
    )
    self_values = pltpu.make_async_copy(
        kv_v.at[1, :, lanes_of(head)], values_own.at[slot_self], local_sem.at[15]
    )
    self_state = pltpu.make_async_copy(
        state_src.at[head], state_all.at[ring, slot_self], local_sem.at[7]
    )
    send_all(q_copy)
    self_q.start()
    farthest_first(send_state)
    state_copy(head_sibling, other, slot_sibling, sibling).start()
    self_state.start()
    send_all(keys_copy)
    self_keys.start()
    send_all(values_copy)
    self_values.start()

    load_hyena.wait()
    product = (hy_v[1].astype(F32) * hy_v[2].astype(F32)).astype(BF16).astype(F32)
    padded[0:positions, :] = jnp.zeros((positions, channels), F32)
    padded[positions:, :] = product
    for load in small[1:]:
        load.wait()
    mixed[...] = skip_v[...] * product
    row_index = lax.broadcasted_iota(jnp.int32, (positions, vocab), 0)
    codes = jnp.zeros((positions, vocab), jnp.int32)
    for t in range(positions):
        codes = jnp.where(row_index == t, bases_s[t], codes)
    codes = jnp.where(row_index == pos_s[0], allele_s[0], codes)
    wanted = jnp.zeros((positions, vocab), jnp.int32)
    for code, token in enumerate(BASE_TOKENS):
        wanted = jnp.where(codes == code, token, wanted)
    targets[...] = wanted

    load_filter.wait()

    def own_taps(h, carry):
        lanes = lanes_of(h)
        coeffs = jnp.transpose(filt_v[lanes, :])
        total = mixed[:, lanes]
        for j in range(1, positions):
            total = total + padded[positions - j : 2 * positions - j, lanes] * coeffs[j - 1 : j, :]
        mixed[:, lanes] = total
        return carry

    lax.fori_loop(0, heads, own_taps, 0)
    taps_own[...] = jnp.transpose(filt_v[lanes_of(head), :])
    state_rows[taps:, :] = jnp.zeros((positions, HEAD_DIM), F32)

    away = (3, n - 3)

    def gather_copy(side):
        return remote(
            q_own,
            gathered.at[side],
            gather_send.at[side],
            gather_recv.at[side],
            ring_device(away[side]),
        )

    wait_for(q_own.at[0 : heads - 1], spread_recv.at[0])
    self_q.wait()
    for side in range(2):
        gather_copy(side).start()

    wait_for(state_all.at[0, 0 : heads - 1], spread_recv.at[1])
    self_state.wait()
    state_mine = state_all.at[ring]

    def send_state_on(k, carry):
        remote(
            state_mine, state_mine, spread_send.at[3], spread_recv.at[3], ring_device(k)
        ).start()
        return carry

    farthest_first(send_state_on)

    right = ring_device(1)
    left = ring_device(n - 1)

    def exchange(ref, send_sem, recv_sem):
        return (
            remote(ref.at[1], ref.at[0], send_sem.at[0], recv_sem.at[0], right),
            remote(ref.at[1], ref.at[2], send_sem.at[1], recv_sem.at[1], left),
        )

    wait_for(keys.at[1, 0 : heads - 1], spread_recv.at[2])
    self_keys.wait()
    keys_on = exchange(keys, keys_send, keys_recv)
    for copy in keys_on:
        copy.start()

    wait_for(values_own.at[0 : heads - 1], spread_recv.at[4])
    self_values.wait()
    block = values_own.shape[1]
    context = heads * block
    values_t[1] = jnp.transpose(values_own[...].reshape(context, HEAD_DIM))
    values_on = exchange(values_t, values_send, values_recv)
    for copy in values_on:
        copy.start()

    wait_for(state_all.at[0 : n - 1], spread_recv.at[3])

    for at in range(n):
        for slot in range(heads):
            spot, bit = divmod(slot, 2)
            row_z = (4 * at + 2 * (spot % 2) + bit) * (n // 2) + spot // 2
            row_y = (4 * spot + 2 * (at % 2) + bit) * (n // 2) + at // 2
            row = row_z + core * (row_y - row_z)
            state_rows[pl.ds(row, 1), :] = state_all[at, slot]

    def state_taps(step, total):
        base = pl.multiple_of(step * 8, 8)
        for b in range(8):
            total = total + (
                state_rows[pl.ds(base + b, positions), :]
                * taps_own[pl.ds(taps - 1 - b - base, 1), :]
            )
        return total

    state_part[...] = lax.fori_loop(
        0, taps // 8, state_taps, jnp.zeros((positions, HEAD_DIM), F32)
    ).astype(BF16)

    def back_device(k, core_to):
        spot = lax.rem(other + k, n)
        return (
            2 * spot + core_to,
            device((1 - core) * z + core * spot, (1 - core) * spot + core * y, core_to),
        )

    slot_beside = 2 * other + 1 - core

    def state_back(device_id):
        return remote(
            state_part, state_parts.at[head], back_send.at[0], back_recv.at[0], device_id
        )

    def send_state_back(k, carry):
        for core_to in range(2):
            state_back(back_device(k, core_to)[1]).start()
        return carry

    farthest_first(send_state_back)
    state_back(sibling).start()
    state_parts[head] = state_part[...]

    def merge(a, b):
        peak = jnp.maximum(a[1], b[1])
        scale_a = jnp.exp2((a[1] - peak) * EXP_SCALE)
        scale_b = jnp.exp2((b[1] - peak) * EXP_SCALE)
        return (a[0] * scale_a + b[0] * scale_b, peak, a[2] * scale_a + b[2] * scale_b)

    def weigh(chunk, place, first=0, last=heads):
        from_keys = keys[place, first:last].reshape((last - first) * block, HEAD_DIM)
        weights, peak, total = [], [], []
        width = min(256, rows)
        for start in range(0, rows, width):
            part = chunk[start : start + width]
            scores = lax.dot_general(
                from_keys, part, (((1,), (1,)), ((), ())), preferred_element_type=F32
            )
            top = jnp.max(scores, 0, keepdims=True)
            weight = jnp.exp2((scores - top) * EXP_SCALE)
            weights.append(weight.astype(BF16))
            peak.append(top)
            total.append(jnp.sum(weight, 0, keepdims=True))
        return [jnp.concatenate(pieces, 1) for pieces in (weights, peak, total)]

    def apply(weights, place, first=0, last=heads):
        from_values = values_t[place, :, first * block : last * block]
        return jnp.dot(from_values, weights, preferred_element_type=F32)

    def attend(chunk, place):
        weights, peak, total = weigh(chunk, place)
        return apply(weights, place), peak, total

    def chunk_of(index):
        ref = q_own if index == 2 else gathered.at[index]
        return ref[...].reshape(rows, HEAD_DIM)

    def store_sums(index, sums):
        sum_numer[index] = sums[0]
        sum_stat[index, 0:1, :] = sums[1]
        sum_stat[index, 1:2, :] = sums[2]

    def load_sums(index):
        return (sum_numer[index], sum_stat[index, 0:1, :], sum_stat[index, 1:2, :])

    for side in range(2):
        gather_copy(side).wait_recv()
        store_sums(side, attend(chunk_of(side), 1))

    def part_copy(side):
        return remote(
            part_out.at[side],
            part_in.at[side],
            part_send.at[side],
            part_recv.at[side],
            ring_device(away[1 - side]),
        )

    def stat_copy(side):
        return remote(
            stat_out.at[side],
            stat_in.at[side],
            stat_send.at[side],
            stat_recv.at[side],
            ring_device(away[1 - side]),
        )

    middle = heads // 2
    spans = (
        ((0, 0, heads), (2, 0, middle)),
        ((2, 0, heads), (0, middle, heads)),
        ((0, 0, heads), (2, 0, heads)),
    )
    for copy in keys_on:
        copy.wait_recv()
    stats = []
    for index in range(2):
        for which, (place, first, last) in enumerate(spans[index]):
            weights, peak, total = weigh(chunk_of(index), place, first, last)
            weights_kept[index, which, 0 : (last - first) * block, :] = weights
            stats.append((peak, total))

    def finish(index):
        sums = load_sums(index)
        for which, (place, first, last) in enumerate(spans[index]):
            numer = apply(
                weights_kept[index, which, 0 : (last - first) * block, :], place, first, last
            )
            sums = merge(sums, (numer, *stats[2 * index + which]))
        return sums

    for copy in values_on:
        copy.wait_recv()
    for side in range(2):
        sums = finish(side)
        part_out[side] = sums[0].astype(BF16)
        stat_out[side, 0:1, :] = sums[1]
        stat_out[side, 1:2, :] = sums[2]
        part_copy(side).start()
        stat_copy(side).start()
    store_sums(2, attend(chunk_of(2), 1))
    for place, first, last in spans[2]:
        store_sums(2, merge(load_sums(2), attend(chunk_of(2), place)))

    mine = load_sums(2)
    for side in range(2):
        part_copy(side).wait_recv()
        stat_copy(side).wait_recv()
        mine = merge(
            mine,
            (part_in[side].astype(F32), stat_in[side, 0:1, :], stat_in[side, 1:2, :]),
        )
    numer, peak, total = mine
    merged[...] = jnp.transpose(numer).astype(BF16).reshape(merged.shape)
    for b in range(rows // HEAD_DIM):
        merged_stat[b, 0:1, :] = peak[:, b * HEAD_DIM : (b + 1) * HEAD_DIM]
        merged_stat[b, 1:2, :] = total[:, b * HEAD_DIM : (b + 1) * HEAD_DIM]

    def back_copy(slot, device_id):
        return remote(
            merged.at[slot], back.at[head], back_send.at[1], back_recv.at[1], device_id
        )

    def back_stat_copy(slot, device_id):
        return remote(
            merged_stat.at[lax.div(slot, group)],
            back_stat.at[head],
            back_send.at[2],
            back_recv.at[2],
            device_id,
        )

    def send_back(k, carry):
        for core_to in range(2):
            slot, device_id = back_device(k, core_to)
            back_copy(slot, device_id).start()
            back_stat_copy(slot, device_id).start()
        return carry

    farthest_first(send_back)
    back_copy(slot_beside, sibling).start()
    back_stat_copy(slot_beside, sibling).start()
    back[head] = merged[slot_self]
    back_stat[head] = merged_stat[lax.div(slot_self, group)]

    wait_for(state_parts.at[0 : heads - 1], back_recv.at[0])
    for h in range(heads):
        lanes = slice(h * HEAD_DIM, (h + 1) * HEAD_DIM)
        hyena_ref[0, :, lanes] = (
            hy_v[0, :, lanes].astype(F32) * (mixed[:, lanes] + state_parts[h].astype(F32))
        ).astype(BF16)
    load_keys.wait()
    own = []
    row_at = lax.broadcasted_iota(jnp.int32, (HEAD_DIM, HEAD_DIM), 0)
    col_at = lax.broadcasted_iota(jnp.int32, (HEAD_DIM, HEAD_DIM), 1)
    seen = (lax.div(row_at, positions) == lax.div(col_at, positions)) & (col_at <= row_at)

    def stacked(ref, g):
        return jnp.concatenate(
            [ref[:, h * HEAD_DIM : (h + 1) * HEAD_DIM] for h in range(g * group, (g + 1) * group)],
            0,
        )

    for g in range(heads // group):
        scores = lax.dot_general(
            stacked(q_v, g), stacked(ck_v, g), (((1,), (1,)), ((), ())), preferred_element_type=F32
        )
        scores = jnp.where(seen, scores, LOWEST)
        top = jnp.max(scores, 1, keepdims=True)
        weights = jnp.where(seen, jnp.exp2((scores - top) * EXP_SCALE), 0.0)
        total = jnp.sum(weights, 1, keepdims=True)
        numer = jnp.dot(
            weights.astype(BF16), stacked(hyena_ref.at[0], g), preferred_element_type=F32
        )
        own.append((numer, top, total))

    load_unembed.wait()
    stat_square[...] = jnp.zeros_like(stat_square)
    wait_for(back_stat.at[0 : heads - 1], back_recv.at[2])
    for first, slot in ((0, slot_y), (n, slot_z)):
        shift = lax.rem(HEAD_DIM - lax.rem(slot, group) * positions, HEAD_DIM)
        for kind in range(2):
            stat_square[kind * heads + first : kind * heads + first + n, :] = pltpu.roll(
                back_stat[first : first + n, kind, :], shift, 1
            )
    columns = jnp.transpose(stat_square[...])
    wait_for(back.at[0 : heads - 1], back_recv.at[1])
    pieces = []
    for g in range(heads // group):
        chosen = range(g * group, (g + 1) * group)
        peak = jnp.concatenate([columns[0:positions, h : h + 1] for h in chosen], 0)
        total = jnp.concatenate(
            [columns[0:positions, heads + h : heads + h + 1] for h in chosen], 0
        )
        numer = back[g * group : (g + 1) * group].reshape(HEAD_DIM, HEAD_DIM).astype(F32)
        numer, _, total = merge((numer, peak, total), own[g])
        attended = numer / total
        pieces += [attended[i * positions : (i + 1) * positions] for i in range(group)]
    attended = jnp.concatenate(pieces, 1)
    high = attended.astype(BF16)
    low = (attended - high.astype(F32)).astype(BF16)
    both = jnp.dot(
        jnp.concatenate([high, low], 0), unembed_v[...], preferred_element_type=F32
    )
    logit_parts[tp] = (both[0:positions] + both[positions:]).astype(BF16)

    tp_copies = [
        remote(
            logit_parts.at[tp],
            logit_parts.at[tp],
            tp_send,
            tp_recv,
            {"tp": lax.rem(tp + k, tp_count)},
        )
        for k in range(1, tp_count)
    ]
    for copy in tp_copies:
        copy.start()
    if tp_count > 1:
        wait_for(logit_parts.at[0 : tp_count - 1], tp_recv)
    logits = logit_parts[0].astype(F32)
    for k in range(1, tp_count):
        logits = logits + logit_parts[k].astype(F32)
    top = jnp.max(logits, 1, keepdims=True)
    log_total = top + jnp.log(jnp.sum(jnp.exp(logits - top), 1, keepdims=True))
    vocab_at = lax.broadcasted_iota(jnp.int32, (positions, vocab), 1)
    picked = jnp.sum(jnp.where(vocab_at == targets[...], logits, 0.0), 1, keepdims=True)
    log_probs = picked - log_total
    place = lax.broadcasted_iota(jnp.int32, (positions, positions), 0)
    lane = lax.broadcasted_iota(jnp.int32, (positions, positions), 1)
    log_row = jnp.sum(jnp.where(place == lane, log_probs, 0.0), 0, keepdims=True)
    log_probs_ref[...] = log_row
    lane_row = lax.broadcasted_iota(jnp.int32, (1, positions), 1)
    score_ref[...] = jnp.sum(
        jnp.where(lane_row < length_s[0], log_row, 0.0), 1, keepdims=True
    )

    wait_for(q_own.at[0 : heads - 1], spread_send.at[0])
    wait_for(state_all.at[0, 0 : heads - 1], spread_send.at[1])
    wait_for(keys.at[1, 0 : heads - 1], spread_send.at[2])
    wait_for(values_own.at[0 : heads - 1], spread_send.at[4])
    wait_for(state_all.at[0 : n - 1], spread_send.at[3])
    for copy in keys_on + values_on:
        copy.wait_send()
    for side in range(2):
        gather_copy(side).wait_send()
        part_copy(side).wait_send()
        stat_copy(side).wait_send()
    wait_for(state_parts.at[0 : heads - 1], back_send.at[0])
    wait_for(back.at[0 : heads - 1], back_send.at[1])
    wait_for(back_stat.at[0 : heads - 1], back_send.at[2])
    if tp_count > 1:
        wait_for(logit_parts.at[0 : tp_count - 1], tp_send)


def on_device(
    n,
    tp_count,
    context_kv,
    queries,
    cont_keys,
    hyena_inputs,
    hyena_state,
    hyena_filter,
    filter_skip,
    unembed,
    ref_bases,
    variant_pos,
    allele_ids,
    cont_lengths,
):
    positions, channels = queries.shape[1:]
    block = context_kv.shape[1]
    taps = hyena_filter.shape[1]
    vocab = unembed.shape[1]
    heads = channels // HEAD_DIM
    rows = heads * positions
    vmem = pltpu.VMEM
    dma = pltpu.SemaphoreType.DMA
    scratch = [
        vmem((heads, positions, HEAD_DIM), BF16),
        vmem((3, heads, block, HEAD_DIM), BF16),
        vmem((heads, block, HEAD_DIM), BF16),
        vmem((3, HEAD_DIM, heads * block), BF16),
        vmem((heads, 1, HEAD_DIM), F32),
        vmem((n, heads, 1, HEAD_DIM), F32),
        vmem((taps + positions, HEAD_DIM), F32),
        vmem((2, heads, positions, HEAD_DIM), BF16),
        vmem((2, HEAD_DIM, rows), BF16),
        vmem((2, 2, rows), F32),
        vmem((2, HEAD_DIM, rows), BF16),
        vmem((2, 2, rows), F32),
        vmem((3, HEAD_DIM, rows), F32),
        vmem((3, 2, rows), F32),
        vmem((3, 2, heads * block, rows), BF16),
        vmem((heads, positions, HEAD_DIM), BF16),
        vmem((rows // HEAD_DIM, 2, HEAD_DIM), F32),
        vmem((heads, positions, HEAD_DIM), BF16),
        vmem((heads, 2, HEAD_DIM), F32),
        vmem((positions, HEAD_DIM), BF16),
        vmem((heads, positions, HEAD_DIM), BF16),
        vmem((HEAD_DIM, HEAD_DIM), F32),
        vmem((tp_count, positions, vocab), BF16),
        vmem((positions, vocab), jnp.int32),
        vmem((2 * positions, channels), F32),
        vmem((positions, channels), F32),
        vmem((taps, HEAD_DIM), F32),
        vmem((positions, channels), BF16),
        vmem((2, block, channels), BF16),
        vmem((positions, channels), BF16),
        vmem((3, positions, channels), BF16),
        vmem((channels, taps), F32),
        vmem((channels, vocab), BF16),
        vmem((1, channels), BF16),
        vmem((1, channels), F32),
        pltpu.SMEM((positions,), jnp.int32),
        pltpu.SMEM((1,), jnp.int32),
        pltpu.SMEM((1,), jnp.int32),
        pltpu.SMEM((1,), jnp.int32),
        dma((16,)),
        dma((5,)),
        dma((5,)),
        dma((2,)),
        dma((2,)),
        dma((2,)),
        dma((2,)),
        dma((2,)),
        dma((2,)),
        dma((2,)),
        dma((2,)),
        dma((2,)),
        dma((2,)),
        dma((3,)),
        dma((3,)),
        dma,
        dma,
    ]
    hbm = pl.BlockSpec(memory_space=pltpu.HBM)
    in_vmem = pl.BlockSpec(memory_space=pltpu.VMEM)
    stay = [
        pltpu.with_memory_space_constraint(array, pltpu.HBM)
        for array in (
            context_kv,
            queries,
            cont_keys,
            hyena_inputs,
            hyena_state,
            hyena_filter,
            filter_skip.reshape(1, channels),
            unembed,
            ref_bases,
        )
    ]
    hyena_out, log_probs, score = pl.pallas_call(
        functools.partial(spread_kernel, n, tp_count),
        out_shape=(
            jax.ShapeDtypeStruct((1, positions, channels), BF16),
            jax.ShapeDtypeStruct((1, positions), F32),
            jax.ShapeDtypeStruct((1, 1), F32),
        ),
        in_specs=[hbm] * 12,
        out_specs=(in_vmem, in_vmem, in_vmem),
        scratch_shapes=scratch,
        compiler_params=pltpu.CompilerParams(
            collective_id=0, has_side_effects=True, vmem_limit_bytes=48 * 1024 * 1024
        ),
    )(
        *stay,
        variant_pos,
        allele_ids,
        cont_lengths,
    )
    return hyena_out, log_probs, score.reshape(1)


def solution(mesh):
    n = mesh.shape["ctx"] // 4
    placed = (
        P(None, ("ctx", "var"), "tp"),
        P(("ctx", "var"), None, "tp"),
        P(("ctx", "var"), None, "tp"),
        P(None, ("ctx", "var"), None, "tp"),
        P(("ctx", "var"), "tp"),
        P("tp", None),
        P("tp"),
        P("tp", None),
        P(),
        P(("ctx", "var")),
        P(("ctx", "var")),
        P(("ctx", "var")),
    )
    return jax.shard_map(
        functools.partial(on_device, n, mesh.shape["tp"]),
        mesh=mesh,
        in_specs=placed,
        out_specs=(P(("ctx", "var"), None, "tp"), P(("ctx", "var"), None), P(("ctx", "var"))),
        check_vma=False,
    )
```
